256 devices in a mesh: grp: 16 (over y, x_lo, core), dev: 16 (over z, x_hi).
Axes of the slice: x: 4 (x_hi: 2, x_lo: 2; x = x_hi * 2 + x_lo), y: 4, z: 8, core: 2. Of those that a mesh axis runs over, the one named last changes fastest.
Arguments:
- hidden: bfloat16 [49152, 2048], P(('grp', 'dev')), may hold values from -60 to 60
- weight: bfloat16 [2048, 128], replicated, may hold values from -0.125 to 0.125
- partner: int32 [49152], P(('grp', 'dev')), may hold values from 0 to 49151, as said below
Outputs:
- mean_loss: float32 [], replicated
- derivative_wrt_inputs: float32 [49152, 128], P(('grp', 'dev'))
- grad_weight: float32 [2048, 128], replicated
The draws below stay inside these ranges and needn't reach their ends.
Inputs may be any that keep to these rules, and one draw needn't show every extreme that they name: partner[partner[i]] = i and partner[i] != i; partner[i] lies in the same aligned block of 192 rows as i.
All inputs are finite; a program needn't handle non-finite values.
Results may differ from the reference program's by a relative error of at most 0.0082.
Values may be sent and summed in bfloat16 or wider, within the bound.
No kernel may reach another device: no remote copies, remote signals or barrier semaphores. Data moves between devices by JAX's collectives and lax.ppermute only.
A program may use at most 128 MiB of HBM per device.

```python
import math
import jax
import jax.numpy as jnp
from jax import lax

D_IN = 2048
D_OUT = 128
ROWS_DEV = 192
TOTAL = 49152


def permuted(single):
    return jax.random.permutation(single, ROWS_DEV)


def pair_layout(key):
    order_key, class_key = jax.random.split(key)
    block_count = TOTAL // ROWS_DEV
    orders = jax.vmap(permuted)(jax.random.split(order_key, block_count)).astype(jnp.int32)
    places = jnp.argsort(orders, axis=1, stable=True).astype(jnp.int32)
    partners = jnp.take_along_axis(orders, places ^ 1, axis=1)
    offsets = (jnp.arange(block_count, dtype=jnp.int32) * ROWS_DEV)[:, None]
    partner_ids = (partners + offsets).reshape(TOTAL).astype(jnp.int32)
    pair_offsets = (jnp.arange(block_count, dtype=jnp.int32) * (ROWS_DEV // 2))[:, None]
    pair_ids = (places // 2 + pair_offsets).reshape(TOTAL).astype(jnp.int32)
    class_count = max(TOTAL // 32, 2)
    pair_classes = jax.random.randint(class_key, (TOTAL // 2,), 0, class_count, dtype=jnp.int32)
    row_classes = jnp.take(pair_classes, pair_ids, axis=0).astype(jnp.int32)
    return (partner_ids, pair_ids, row_classes)


def draw_hidden(key, part):
    unused, pair_ids, row_classes = pair_layout(key)
    key = jax.random.fold_in(key, 11)
    centre_key, pair_key, view_key = jax.random.split(key, 3)
    class_count = max(TOTAL // 32, 2)
    centres = jnp.clip(jax.random.normal(centre_key, (class_count, D_IN), jnp.float32), -4.0, 4.0)
    pair_noise = jnp.clip(jax.random.normal(pair_key, (TOTAL // 2, D_IN), jnp.float32), -4.0, 4.0)
    view_noise = jnp.clip(jax.random.normal(view_key, (TOTAL, D_IN), jnp.float32), -4.0, 4.0)
    values = 0.9 * jnp.take(centres, row_classes, axis=0) + 0.35 * jnp.take(pair_noise, pair_ids, axis=0) + 0.25 * view_noise
    return values.astype(jnp.bfloat16)


def draw_partner(key, part):
    partner_ids, unused, others = pair_layout(key)
    return partner_ids.astype(jnp.int32)


def gaussian(rng, extent, deviation, reach, held_as=jnp.bfloat16):
    array = jax.random.normal(rng, extent, jnp.float32) * deviation
    return jnp.minimum(jnp.maximum(array, -reach), reach).astype(held_as)


def setup_inputs(seed: int = 0) -> dict:
    arg_keys = jax.random.split(jax.random.key(seed), 4)
    return {
        "hidden": draw_hidden(jax.random.fold_in(arg_keys[3], 71), 0),
        "weight": gaussian(arg_keys[1], (D_IN, D_OUT), D_IN ** -0.5, 0.125),
        "partner": draw_partner(jax.random.fold_in(arg_keys[3], 71), 0),
    }


inverse_tau = 10.0
norm_epsilon = 1e-06

def reference(hidden, weight, partner):
    projected = jnp.dot(hidden, weight, preferred_element_type=jnp.float32)
    inverse_norm = lax.rsqrt(lax.optimization_barrier(jnp.sum(projected * projected, axis=1, keepdims=True)) + norm_epsilon)
    unit_rows = projected * inverse_norm
    encoded_vectors = unit_rows.astype(jnp.bfloat16)
    block_size = math.gcd(TOTAL, 512)
    block_count = TOTAL // block_size
    column_ids = jnp.arange(TOTAL, dtype=jnp.int32)

    def block_scores(block_index):
        first_row = block_index * block_size
        entry_tile = lax.dynamic_slice_in_dim(encoded_vectors, first_row, block_size, 0)
        scaled_cosine_matrix = inverse_tau * lax.dot_general(entry_tile, encoded_vectors, (((1,), (1,)), ((), ())), preferred_element_type=jnp.float32)
        own_ids = first_row + jnp.arange(block_size, dtype=jnp.int32)
        return (scaled_cosine_matrix, own_ids[:, None] != column_ids[None, :])

    def row_sums(block_index):
        scaled_cosine_matrix, kept_indicator = block_scores(block_index)
        return lax.optimization_barrier(jnp.sum(jnp.where(kept_indicator, jnp.exp(scaled_cosine_matrix - inverse_tau), 0.0), axis=1))
    block_ids = jnp.arange(block_count, dtype=jnp.int32)
    overall_partition_totals = lax.map(row_sums, block_ids).reshape(TOTAL)
    normalizer_logarithms = inverse_tau + jnp.log(overall_partition_totals)

    def weighted(block_index):
        scaled_cosine_matrix, kept_indicator = block_scores(block_index)
        own_logs = lax.dynamic_slice_in_dim(normalizer_logarithms, block_index * block_size, block_size, 0)
        combined = jnp.exp(scaled_cosine_matrix - own_logs[:, None]) + jnp.exp(scaled_cosine_matrix - normalizer_logarithms[None, :])
        mixing = jnp.where(kept_indicator, combined, 0.0).astype(jnp.bfloat16)
        return jnp.dot(mixing, encoded_vectors, preferred_element_type=jnp.float32)
    probability_combined_vector = lax.map(weighted, block_ids).reshape(TOTAL, D_OUT)
    partner_vectors = jnp.take(encoded_vectors, partner, axis=0).astype(jnp.float32)
    paired_scaled_score = inverse_tau * lax.optimization_barrier(jnp.sum(encoded_vectors.astype(jnp.float32) * partner_vectors, axis=1))
    mean_loss = jnp.sum(normalizer_logarithms - paired_scaled_score) / TOTAL
    derivative_wrt_inputs = inverse_tau * (probability_combined_vector - 2.0 * partner_vectors)
    alongside = lax.optimization_barrier(jnp.sum(unit_rows * derivative_wrt_inputs, axis=1, keepdims=True))
    projected_grad = ((derivative_wrt_inputs - unit_rows * alongside) * inverse_norm).astype(jnp.bfloat16)
    grad_weight = jnp.dot(hidden.T, projected_grad, preferred_element_type=jnp.float32)
    return (mean_loss, derivative_wrt_inputs, grad_weight)
```

```python
import jax
import jax.numpy as jnp
from jax import lax
from jax.experimental import pallas as pl
from jax.experimental.pallas import tpu as pltpu
from jax.sharding import Mesh
from jax.sharding import PartitionSpec as P

inverse_tau = 10.0
norm_epsilon = 1e-06
log2_e = 1.4426950408889634

AXES = ("y", "xl", "c", "z", "xh")
PLANE = ("y", "xl", "xh")
ROWS = 192
WIDTH = 128
D_IN = 2048
HALF = 8 * ROWS
SPAN = 16 * ROWS
BLOCK = 384
CHUNK = 256
VMEM_BYTES = 56 * 1024 * 1024


def params():
    return pltpu.CompilerParams(vmem_limit_bytes=VMEM_BYTES)


def whole(shape):
    return pl.BlockSpec(shape, lambda *_: (0,) * len(shape))


def project_body(hidden_ref, weight_ref, partner_ref, projected_ref, features_ref, pair_ref, pair_sum_ref):
    projected = jnp.dot(hidden_ref[...], weight_ref[...], preferred_element_type=jnp.float32)
    inverse_norm = lax.rsqrt(jnp.sum(projected * projected, axis=1, keepdims=True) + norm_epsilon)
    features = (projected * inverse_norm).astype(jnp.bfloat16)
    places = lax.rem(partner_ref[...], ROWS)
    picks = lax.broadcasted_iota(jnp.int32, (ROWS, ROWS), 0) == places
    paired = jnp.dot(
        jnp.where(picks, 1.0, 0.0).astype(jnp.bfloat16), features, preferred_element_type=jnp.float32
    )
    projected_ref[...] = projected
    features_ref[...] = features
    pair_ref[...] = paired
    products = features.astype(jnp.float32) * paired
    total = jnp.sum(jnp.sum(products, axis=1, keepdims=True), axis=0, keepdims=True)
    pair_sum_ref[...] = jnp.broadcast_to(inverse_tau * total, (8, WIDTH))


def project(hidden, weight, partner):
    return pl.pallas_call(
        project_body,
        out_shape=(
            jax.ShapeDtypeStruct((ROWS, WIDTH), jnp.float32),
            jax.ShapeDtypeStruct((ROWS, WIDTH), jnp.bfloat16),
            jax.ShapeDtypeStruct((ROWS, WIDTH), jnp.float32),
            jax.ShapeDtypeStruct((8, WIDTH), jnp.float32),
        ),
        compiler_params=params(),
        name="project",
    )(hidden, weight, partner.reshape(1, ROWS))


def score_body(place_ref, own_ref, other_ref, columns_ref, pair_sum_ref, powers_ref, sums_ref, turned, running):
    step = pl.program_id(0)
    own_steps = HALF // BLOCK

    @pl.when(step == 0)
    def _():
        for n in range(SPAN // CHUNK):
            piece = jnp.transpose(columns_ref[pl.ds(n * CHUNK, CHUNK), :])
            turned[0:WIDTH, pl.ds(n * CHUNK, CHUNK)] = piece
            turned[WIDTH : 2 * WIDTH, pl.ds(n * CHUNK, CHUNK)] = piece
        running[...] = jnp.zeros_like(running)

    first = lax.rem(step, own_steps) * BLOCK
    rows = jnp.where(
        step < own_steps,
        own_ref[pl.ds(first, BLOCK), :].astype(jnp.float32),
        other_ref[pl.ds(first, BLOCK), :].astype(jnp.float32),
    )
    scaled = rows * (inverse_tau * log2_e)
    high = scaled.astype(jnp.bfloat16)
    low = (scaled - high.astype(jnp.float32)).astype(jnp.bfloat16)
    left = jnp.concatenate([high, low], axis=1)

    def fill(masked):
        for n in range(SPAN // CHUNK):
            columns = pl.ds(n * CHUNK, CHUNK)
            powers = jnp.exp2(jnp.dot(left, turned[:, columns], preferred_element_type=jnp.float32))
            if masked:
                own_row = first + lax.broadcasted_iota(jnp.int32, (BLOCK, CHUNK), 0) - place_ref[0] * ROWS
                own_column = n * CHUNK + lax.broadcasted_iota(jnp.int32, (BLOCK, CHUNK), 1) - place_ref[1] * ROWS
                same = (own_row == own_column) & (own_row >= 0) & (own_row < ROWS)
                powers = jnp.where(same, 0.0, powers)
            powers_ref[:, columns] = powers.astype(jnp.bfloat16)
            running[:, columns] += jnp.sum(powers.reshape(BLOCK // 8, 8, CHUNK), axis=0)

    masked_step = (step < own_steps) & (first <= place_ref[0] * ROWS) & (place_ref[0] * ROWS < first + BLOCK)
    pl.when(masked_step)(lambda: fill(True))
    pl.when(jnp.logical_not(masked_step))(lambda: fill(False))

    @pl.when(step == pl.num_programs(0) - 1)
    def _():
        sums = jnp.sum(running[...], axis=0, keepdims=True)
        for k in range(SPAN // WIDTH):
            sums_ref[k : k + 1, :] = sums[:, k * WIDTH : (k + 1) * WIDTH]
        sums_ref[SPAN // WIDTH :, :] = pair_sum_ref[...]


def score(place, own, other, columns, pair_sum):
    return pl.pallas_call(
        score_body,
        grid=(SPAN // BLOCK,),
        in_specs=[
            pl.BlockSpec(memory_space=pltpu.SMEM),
            whole((HALF, WIDTH)),
            whole((HALF, WIDTH)),
            whole((SPAN, WIDTH)),
            whole((8, WIDTH)),
        ],
        out_specs=(
            pl.BlockSpec((BLOCK, SPAN), lambda i: (i, 0)),
            whole((SPAN // WIDTH + 8, WIDTH)),
        ),
        out_shape=(
            jax.ShapeDtypeStruct((SPAN, SPAN), jnp.bfloat16),
            jax.ShapeDtypeStruct((SPAN // WIDTH + 8, WIDTH), jnp.float32),
        ),
        scratch_shapes=[
            pltpu.VMEM((2 * WIDTH, SPAN), jnp.bfloat16),
            pltpu.VMEM((8, SPAN), jnp.float32),
        ],
        compiler_params=params(),
        name="score",
    )(place, own, other, columns, pair_sum)


def weigh_other_body(place_ref, partial_ref, columns_ref, powers_ref, out_ref, both_ref, own_ref, loss_ref, inverse):
    @pl.when(pl.program_id(0) == 0)
    def _():
        tiles = SPAN // WIDTH
        sums = jnp.sum(partial_ref[...], axis=0)
        totals = sums[:tiles, :]
        loss = jnp.sum(jnp.sum(jnp.log(totals), axis=1, keepdims=True), axis=0, keepdims=True)
        loss_ref[...] = loss - sums[tiles:, :]
        inverses = 1.0 / totals
        for k in range(tiles):
            rows = pl.ds(k * WIDTH, WIDTH)
            turned = jnp.transpose(jnp.broadcast_to(inverses[k : k + 1, :], (WIDTH, WIDTH)))
            inverse[rows, :] = turned
            piece = columns_ref[rows, :]
            both_ref[rows, 0:WIDTH] = piece
            both_ref[rows, WIDTH : 2 * WIDTH] = (piece.astype(jnp.float32) * turned).astype(jnp.bfloat16)
        own_ref[...] = inverse[pl.ds(pl.multiple_of(place_ref[1] * ROWS, ROWS), ROWS), :]

    out_ref[...] = jnp.dot(
        powers_ref[...], both_ref[...], preferred_element_type=jnp.float32
    ).astype(jnp.bfloat16)


def weigh_other(place, partial, columns, powers):
    return pl.pallas_call(
        weigh_other_body,
        grid=(HALF // BLOCK,),
        in_specs=[
            pl.BlockSpec(memory_space=pltpu.SMEM),
            whole(partial.shape),
            whole((SPAN, WIDTH)),
            pl.BlockSpec((BLOCK, SPAN), lambda i: (i + HALF // BLOCK, 0)),
        ],
        out_specs=(
            pl.BlockSpec((BLOCK, 2 * WIDTH), lambda i: (i, 0)),
            whole((SPAN, 2 * WIDTH)),
            whole((ROWS, WIDTH)),
            whole((8, WIDTH)),
        ),
        out_shape=(
            jax.ShapeDtypeStruct((HALF, 2 * WIDTH), jnp.bfloat16),
            jax.ShapeDtypeStruct((SPAN, 2 * WIDTH), jnp.bfloat16),
            jax.ShapeDtypeStruct((ROWS, WIDTH), jnp.float32),
            jax.ShapeDtypeStruct((8, WIDTH), jnp.float32),
        ),
        scratch_shapes=[pltpu.VMEM((SPAN, WIDTH), jnp.float32)],
        compiler_params=params(),
        name="weigh_other",
    )(place, partial, columns, powers)


def weigh_own_body(both_ref, powers_ref, out_ref):
    out_ref[...] = jnp.dot(powers_ref[...], both_ref[...], preferred_element_type=jnp.float32)


def weigh_own(both, powers):
    return pl.pallas_call(
        weigh_own_body,
        grid=(HALF // BLOCK,),
        in_specs=[
            whole((SPAN, 2 * WIDTH)),
            pl.BlockSpec((BLOCK, SPAN), lambda i: (i, 0)),
        ],
        out_specs=pl.BlockSpec((BLOCK, 2 * WIDTH), lambda i: (i, 0)),
        out_shape=jax.ShapeDtypeStruct((HALF, 2 * WIDTH), jnp.float32),
        compiler_params=params(),
        name="weigh_own",
        cost_estimate=pl.CostEstimate(
            flops=2 * HALF * SPAN * 2 * WIDTH, bytes_accessed=2 * HALF * SPAN, transcendentals=0
        ),
    )(both, powers)


def gradient_body(core_ref, arrived_ref, inverse_ref, pair_ref, projected_ref, hidden_ref, derivative_ref, own_ref, other_ref):
    sums = jnp.sum(arrived_ref[...].astype(jnp.float32), axis=0)
    mixed = inverse_ref[...] * sums[:, :WIDTH] + sums[:, WIDTH:]
    derivative = inverse_tau * (mixed - 2.0 * pair_ref[...])
    derivative_ref[...] = derivative
    projected = projected_ref[...]
    inverse_norm = lax.rsqrt(jnp.sum(projected * projected, axis=1, keepdims=True) + norm_epsilon)
    unit = projected * inverse_norm
    alongside = jnp.sum(unit * derivative, axis=1, keepdims=True)
    projected_grad = ((derivative - unit * alongside) * inverse_norm).astype(jnp.bfloat16)
    share = D_IN // 2
    for half in range(2):
        product = lax.dot_general(
            hidden_ref[:, half * share : (half + 1) * share],
            projected_grad,
            (((0,), (0,)), ((), ())),
            preferred_element_type=jnp.float32,
        )

        @pl.when(core_ref[0] == half)
        def _():
            own_ref[...] = product

        @pl.when(core_ref[0] != half)
        def _():
            other_ref[...] = product.astype(jnp.bfloat16)


def gradient(core, arrived, inverse, pair, projected, hidden):
    vmem = pl.BlockSpec(memory_space=pltpu.VMEM)
    return pl.pallas_call(
        gradient_body,
        in_specs=[pl.BlockSpec(memory_space=pltpu.SMEM)] + [vmem] * 5,
        out_shape=(
            jax.ShapeDtypeStruct((ROWS, WIDTH), jnp.float32),
            jax.ShapeDtypeStruct((D_IN // 2, WIDTH), jnp.float32),
            jax.ShapeDtypeStruct((D_IN // 2, WIDTH), jnp.bfloat16),
        ),
        compiler_params=params(),
        name="gradient",
    )(core, arrived, inverse, pair, projected, hidden)


def swapped(value):
    return lax.ppermute(value, "c", [(0, 1), (1, 0)])


def spread(value, axes, count):
    copies = jnp.broadcast_to(value[None], (count, *value.shape))
    return lax.all_to_all(copies, axes, 0, 0)


def local(hidden, weight, partner):
    core = lax.axis_index("c").astype(jnp.int32).reshape(1)
    plane_place = (lax.axis_index("y") * 2 + lax.axis_index("xl")) * 2 + lax.axis_index("xh")
    place = jnp.stack([lax.axis_index("z"), plane_place]).astype(jnp.int32)

    projected, features, pair, pair_sum = project(hidden, weight, partner)
    own = spread(features, "z", 8).reshape(HALF, WIDTH)
    other = swapped(own)
    columns = spread(features, PLANE, 16).reshape(SPAN, WIDTH)

    powers, sums = score(place, own, other, columns, pair_sum)
    partial = spread(sums, PLANE, 16)
    other_weighed, both, inverse, loss = weigh_other(place, partial, columns, powers)
    other_arrived = swapped(other_weighed)
    loss = loss + swapped(loss)
    own_weighed = weigh_own(both, powers)
    combined = (own_weighed + other_arrived.astype(jnp.float32)).astype(jnp.bfloat16)
    arrived = lax.all_to_all(combined.reshape(8, ROWS, 2 * WIDTH), "z", 0, 0)

    derivative, own_grad, other_grad = gradient(core, arrived, inverse, pair, projected, hidden)
    half_grad = (own_grad + swapped(other_grad).astype(jnp.float32)).astype(jnp.bfloat16)
    shares = lax.all_to_all(half_grad.reshape(16, 64, WIDTH), PLANE, 0, 0)
    share = jnp.sum(shares.astype(jnp.float32), axis=0)
    summed = jnp.sum(spread(jnp.concatenate([share, loss], axis=0), "z", 8), axis=0)
    mean_loss = summed[64, 0] / (256 * ROWS)
    own_part = spread(summed[:64].astype(jnp.bfloat16), PLANE, 16).reshape(D_IN // 2, WIDTH)
    other_part = swapped(own_part)
    first = jnp.where(core[0] == 0, own_part, other_part)
    second = jnp.where(core[0] == 0, other_part, own_part)
    grad_weight = jnp.concatenate([first, second], axis=0).astype(jnp.float32)
    return (mean_loss, derivative, grad_weight)


def solution(mesh):
    split = Mesh(mesh.devices.reshape(4, 2, 2, 8, 2), AXES)
    return jax.shard_map(
        local,
        mesh=split,
        in_specs=(P(AXES, None), P(), P(AXES)),
        out_specs=(P(), P(AXES, None), P()),
        check_vma=False,
    )
```

```python
import jax
import jax.numpy as jnp
from jax import lax
from jax.experimental import pallas as pl
from jax.experimental.pallas import tpu as pltpu
from jax.sharding import Mesh
from jax.sharding import PartitionSpec as P

inverse_tau = 10.0
norm_epsilon = 1e-06
log2_e = 1.4426950408889634

AXES = ("y", "xl", "c", "z", "xh")
PLANE = ("y", "xl", "xh")
COLUMN = ("z", "c")
WIDE = ("y", "xl", "xh", "c")
ROWS = 192
WIDTH = 128
D_IN = 2048
SPAN = 16 * ROWS
TILES = SPAN // WIDTH
SHARE = D_IN // 32
MEBI = 1024 * 1024

VMEM = pl.BlockSpec(memory_space=pltpu.VMEM)
SMEM = pl.BlockSpec(memory_space=pltpu.SMEM)


def params(size):
    return pltpu.CompilerParams(vmem_limit_bytes=size * MEBI)


def total_of(values):
    return jnp.sum(jnp.sum(values, axis=1, keepdims=True), axis=0, keepdims=True)


def project_body(hidden_ref, weight_ref, partner_ref, projected_ref, features_ref, copies_ref, pair_ref, pair_sum_ref):
    projected = jnp.dot(hidden_ref[...], weight_ref[...], preferred_element_type=jnp.float32)
    inverse_norm = lax.rsqrt(jnp.sum(projected * projected, axis=1, keepdims=True) + norm_epsilon)
    features = (projected * inverse_norm).astype(jnp.bfloat16)
    features_ref[...] = features
    for k in range(16):
        copies_ref[k] = features
    places = lax.rem(partner_ref[...], ROWS)
    picks = lax.broadcasted_iota(jnp.int32, (ROWS, ROWS), 0) == places
    paired = jnp.dot(
        jnp.where(picks, 1.0, 0.0).astype(jnp.bfloat16), features, preferred_element_type=jnp.float32
    )
    projected_ref[...] = projected
    pair_ref[...] = paired
    total = total_of(features.astype(jnp.float32) * paired)
    pair_sum_ref[...] = jnp.broadcast_to(inverse_tau * total, (8, WIDTH))


def project(hidden, weight, partner):
    return pl.pallas_call(
        project_body,
        in_specs=[VMEM] * 3,
        out_specs=(VMEM,) * 5,
        out_shape=(
            jax.ShapeDtypeStruct((ROWS, WIDTH), jnp.float32),
            jax.ShapeDtypeStruct((ROWS, WIDTH), jnp.bfloat16),
            pltpu.VMEM((16, ROWS, WIDTH), jnp.bfloat16),
            jax.ShapeDtypeStruct((ROWS, WIDTH), jnp.float32),
            jax.ShapeDtypeStruct((8, WIDTH), jnp.float32),
        ),
        compiler_params=params(8),
        name="project",
    )(hidden, weight, partner.reshape(1, ROWS))


def score_body(place_ref, rows_ref, columns_ref, pair_sum_ref, powers_ref, sums_ref, left, right):
    for b in range(16):
        shard = rows_ref[lax.rem(place_ref[0] + b, 16)]
        scaled = shard.astype(jnp.float32) * (inverse_tau * log2_e)
        high = scaled.astype(jnp.bfloat16)
        left[b * ROWS : (b + 1) * ROWS, :WIDTH] = high
        left[b * ROWS : (b + 1) * ROWS, WIDTH:] = (scaled - high.astype(jnp.float32)).astype(jnp.bfloat16)
    chunk = 2 * WIDTH
    for n in range(SPAN // chunk):
        columns = slice(n * chunk, (n + 1) * chunk)
        piece = jnp.transpose(columns_ref[columns, :])
        right[:WIDTH, columns] = piece
        right[WIDTH:, columns] = piece
    for n in range(SPAN // chunk):
        columns = slice(n * chunk, (n + 1) * chunk)
        powers = jnp.exp2(jnp.dot(left[...], right[:, columns], preferred_element_type=jnp.float32))
        own_row = lax.broadcasted_iota(jnp.int32, (ROWS, chunk), 0) + place_ref[1] * ROWS
        own_column = lax.broadcasted_iota(jnp.int32, (ROWS, chunk), 1) + n * chunk
        first = jnp.where(own_row == own_column, 0.0, powers[:ROWS, :])
        rest = powers[ROWS:, :]
        powers_ref[:ROWS, columns] = first.astype(jnp.bfloat16)
        powers_ref[ROWS:, columns] = rest.astype(jnp.bfloat16)
        sums = jnp.sum(first.reshape(ROWS // 8, 8, chunk), axis=0)
        sums += jnp.sum(rest.reshape((SPAN - ROWS) // 8, 8, chunk), axis=0)
        sums = jnp.sum(sums, axis=0, keepdims=True)
        for half in range(2):
            part = jnp.broadcast_to(sums[:, half * WIDTH : (half + 1) * WIDTH].reshape(1, 1, WIDTH), (16, 1, WIDTH))
            sums_ref[:, 2 * n + half : 2 * n + half + 1, :] = part
    sums_ref[:, TILES:, :] = jnp.broadcast_to(pair_sum_ref[...].reshape(1, 8, WIDTH), (16, 8, WIDTH))


def score(place, rows, columns, pair_sum):
    return pl.pallas_call(
        score_body,
        in_specs=[SMEM] + [VMEM] * 3,
        out_specs=(VMEM, VMEM),
        out_shape=(
            pltpu.VMEM((SPAN, SPAN), jnp.bfloat16),
            pltpu.VMEM((16, TILES + 8, WIDTH), jnp.float32),
        ),
        scratch_shapes=[
            pltpu.VMEM((SPAN, 2 * WIDTH), jnp.bfloat16),
            pltpu.VMEM((2 * WIDTH, SPAN), jnp.bfloat16),
        ],
        compiler_params=params(20),
        name="score",
    )(place, rows, columns, pair_sum)


def weigh_body(place_ref, partial_ref, columns_ref, powers_ref, out_ref, own_ref, loss_ref, inverse, both):
    sums = jnp.sum(partial_ref[...], axis=0)
    totals = sums[:TILES, :]
    loss_ref[...] = total_of(jnp.log(totals)) - sums[TILES:, :]
    inverses = 1.0 / totals
    for k in range(TILES):
        rows = slice(k * WIDTH, (k + 1) * WIDTH)
        turned = jnp.transpose(jnp.broadcast_to(inverses[k : k + 1, :], (WIDTH, WIDTH)))
        inverse[rows, :] = turned
        piece = columns_ref[rows, :]
        both[rows, :WIDTH] = piece
        both[rows, WIDTH:] = (piece.astype(jnp.float32) * turned).astype(jnp.bfloat16)
    own_ref[...] = inverse[pl.ds(pl.multiple_of(place_ref[1] * ROWS, ROWS), ROWS), :]
    block = 4 * ROWS
    for i in range(SPAN // block):
        weighed = jnp.dot(
            powers_ref[i * block : (i + 1) * block, :], both[...], preferred_element_type=jnp.float32
        ).astype(jnp.bfloat16)
        for b in range(4):
            out_ref[lax.rem(place_ref[0] + 4 * i + b, 16)] = weighed[b * ROWS : (b + 1) * ROWS, :]


def weigh(place, partial, columns, powers):
    return pl.pallas_call(
        weigh_body,
        in_specs=[SMEM] + [VMEM] * 3,
        out_specs=(VMEM,) * 3,
        out_shape=(
            pltpu.VMEM((16, ROWS, 2 * WIDTH), jnp.bfloat16),
            jax.ShapeDtypeStruct((ROWS, WIDTH), jnp.float32),
            jax.ShapeDtypeStruct((8, WIDTH), jnp.float32),
        ),
        scratch_shapes=[
            pltpu.VMEM((SPAN, WIDTH), jnp.float32),
            pltpu.VMEM((SPAN, 2 * WIDTH), jnp.bfloat16),
        ],
        compiler_params=params(20),
        name="weigh",
    )(place, partial, columns, powers)


def gradient_body(arrived_ref, inverse_ref, pair_ref, projected_ref, hidden_ref, derivative_ref, grad_ref):
    sums = jnp.sum(arrived_ref[...].astype(jnp.float32), axis=0)
    mixed = inverse_ref[...] * sums[:, :WIDTH] + sums[:, WIDTH:]
    derivative = inverse_tau * (mixed - 2.0 * pair_ref[...])
    derivative_ref[...] = derivative
    projected = projected_ref[...]
    inverse_norm = lax.rsqrt(jnp.sum(projected * projected, axis=1, keepdims=True) + norm_epsilon)
    unit = projected * inverse_norm
    alongside = jnp.sum(unit * derivative, axis=1, keepdims=True)
    projected_grad = ((derivative - unit * alongside) * inverse_norm).astype(jnp.bfloat16)
    grad_ref[...] = lax.dot_general(
        hidden_ref[...], projected_grad, (((0,), (0,)), ((), ())), preferred_element_type=jnp.float32
    ).astype(jnp.bfloat16)


def gradient(arrived, inverse, pair, projected, hidden):
    return pl.pallas_call(
        gradient_body,
        in_specs=[VMEM] * 5,
        out_specs=(VMEM, VMEM),
        out_shape=(
            jax.ShapeDtypeStruct((ROWS, WIDTH), jnp.float32),
            pltpu.VMEM((D_IN, WIDTH), jnp.bfloat16),
        ),
        compiler_params=params(16),
        name="gradient",
    )(arrived, inverse, pair, projected, hidden)


def share_body(arrived_ref, copies_ref):
    total = jnp.sum(arrived_ref[...].astype(jnp.float32), axis=0)
    for k in range(8):
        copies_ref[k] = total


def share(arrived):
    return pl.pallas_call(
        share_body,
        in_specs=[VMEM],
        out_specs=VMEM,
        out_shape=pltpu.VMEM((8, SHARE, WIDTH), jnp.float32),
        compiler_params=params(8),
        name="share",
    )(arrived)


def packet_body(arrived_ref, loss_ref, copies_ref):
    total = jnp.sum(arrived_ref[...], axis=0).astype(jnp.bfloat16)
    loss = jnp.broadcast_to(loss_ref[0:1, :], (16, WIDTH))
    high = loss.astype(jnp.bfloat16).astype(jnp.float32)
    middle = (loss - high).astype(jnp.bfloat16).astype(jnp.float32)
    low = loss - high - middle
    row = lax.broadcasted_iota(jnp.int32, (16, WIDTH), 0)
    pieces = jnp.where(row == 0, high, jnp.where(row == 1, middle, jnp.where(row == 2, low, 0.0)))
    pieces = pieces.astype(jnp.bfloat16)
    for k in range(32):
        copies_ref[k, :SHARE, :] = total
        copies_ref[k, SHARE:, :] = pieces


def packet(arrived, loss):
    return pl.pallas_call(
        packet_body,
        in_specs=[VMEM] * 2,
        out_specs=VMEM,
        out_shape=pltpu.VMEM((32, SHARE + 16, WIDTH), jnp.bfloat16),
        compiler_params=params(8),
        name="packet",
    )(arrived, loss)


def finish_body(arrived_ref, loss_ref, grad_ref):
    for k in range(32):
        grad_ref[k] = arrived_ref[k, :SHARE, :].astype(jnp.float32)
    pieces = jnp.sum(arrived_ref[:, SHARE:, :].astype(jnp.float32), axis=0)
    loss_ref[...] = jnp.sum(pieces[:, 0:1], axis=0, keepdims=True) * (0.5 / (256 * ROWS))


def finish(arrived):
    return pl.pallas_call(
        finish_body,
        in_specs=[VMEM],
        out_specs=(VMEM, VMEM),
        out_shape=(
            jax.ShapeDtypeStruct((1, 1), jnp.float32),
            jax.ShapeDtypeStruct((32, SHARE, WIDTH), jnp.float32),
        ),
        compiler_params=params(8),
        name="finish",
    )(arrived)


def local(hidden, weight, partner):
    plane_place = (lax.axis_index("y") * 2 + lax.axis_index("xl")) * 2 + lax.axis_index("xh")
    column_place = lax.axis_index("z") * 2 + lax.axis_index("c")
    place = jnp.stack([plane_place, column_place]).astype(jnp.int32)

    projected, features, copies, pair, pair_sum = project(hidden, weight, partner)
    columns = lax.all_gather(features, COLUMN, axis=0, tiled=True)
    rows = lax.all_to_all(copies, PLANE, 0, 0)
    powers, sums = score(place, rows, columns, pair_sum)
    partial = lax.all_to_all(sums, COLUMN, 0, 0)
    weighed, inverse, loss = weigh(place, partial, columns, powers)
    arrived = lax.all_to_all(weighed, PLANE, 0, 0)
    derivative, grad = gradient(arrived, inverse, pair, projected, hidden)
    shares = lax.all_to_all(grad.reshape(32, SHARE, WIDTH), WIDE, 0, 0)
    shares = lax.all_to_all(share(shares), "z", 0, 0)
    packets = lax.all_to_all(packet(shares, loss), WIDE, 0, 0)
    mean_loss, grad_weight = finish(packets)
    return (mean_loss.reshape(()), derivative, grad_weight.reshape(D_IN, WIDTH))


def solution(mesh):
    split = Mesh(mesh.devices.reshape(4, 2, 2, 8, 2), AXES)
    return jax.shard_map(
        local,
        mesh=split,
        in_specs=(P(AXES, None), P(), P(AXES)),
        out_specs=(P(), P(AXES, None), P()),
        check_vma=False,
    )
```

```python
import jax
import jax.numpy as jnp
from jax import lax
from jax.experimental import pallas as pl
from jax.experimental.pallas import tpu as pltpu
from jax.sharding import Mesh
from jax.sharding import PartitionSpec as P

inverse_tau = 10.0
norm_epsilon = 1e-06
log2_e = 1.4426950408889634

AXES = ("y", "xl", "c", "z", "xh")
PLANE = ("y", "xl", "xh")
COLUMN = ("z", "c")
ROWS = 192
WIDTH = 128
D_IN = 2048
SPAN = 16 * ROWS
TILES = SPAN // WIDTH
SHARE = D_IN // 32
HALF = D_IN // 2
PIECES = 2
MEBI = 1024 * 1024

VMEM = pl.BlockSpec(memory_space=pltpu.VMEM)
SMEM = pl.BlockSpec(memory_space=pltpu.SMEM)
ANY = pl.BlockSpec(memory_space=pl.ANY)


def params(size):
    return pltpu.CompilerParams(vmem_limit_bytes=size * MEBI)


def total_of(values):
    return jnp.sum(jnp.sum(values, axis=1, keepdims=True), axis=0, keepdims=True)


def project_body(
    hidden_hbm, weight_hbm, partner_hbm, projected_ref, features_ref, copies_ref, pair_ref, pair_sum_ref,
    hidden, weight, partner, hidden_done, weight_done, partner_done,
):
    depth = D_IN // PIECES
    copies = []
    for k in range(PIECES):
        part = slice(k * depth, (k + 1) * depth)
        copies.append(
            (
                pltpu.make_async_copy(hidden_hbm.at[:, part], hidden.at[:, part], hidden_done.at[k]),
                pltpu.make_async_copy(weight_hbm.at[part, :], weight.at[part, :], weight_done.at[k]),
            )
        )
    partner_copy = pltpu.make_async_copy(partner_hbm, partner, partner_done)
    for first, second in copies:
        first.start()
        second.start()
    partner_copy.start()
    projected = jnp.zeros((ROWS, WIDTH), jnp.float32)
    for k in range(PIECES):
        part = slice(k * depth, (k + 1) * depth)
        for copy in copies[k]:
            copy.wait()
        projected += jnp.dot(hidden[:, part], weight[part, :], preferred_element_type=jnp.float32)
    inverse_norm = lax.rsqrt(jnp.sum(projected * projected, axis=1, keepdims=True) + norm_epsilon)
    features = (projected * inverse_norm).astype(jnp.bfloat16)
    features_ref[...] = features
    for k in range(16):
        copies_ref[k] = features
    partner_copy.wait()
    places = lax.rem(partner[...], ROWS)
    picks = lax.broadcasted_iota(jnp.int32, (ROWS, ROWS), 0) == places
    paired = jnp.dot(
        jnp.where(picks, 1.0, 0.0).astype(jnp.bfloat16), features, preferred_element_type=jnp.float32
    )
    projected_ref[...] = projected
    pair_ref[...] = paired
    total = total_of(features.astype(jnp.float32) * paired)
    pair_sum_ref[...] = jnp.broadcast_to(inverse_tau * total, (8, WIDTH))


def project(hidden, weight, partner):
    return pl.pallas_call(
        project_body,
        in_specs=[ANY] * 3,
        out_specs=(VMEM,) * 5,
        out_shape=(
            jax.ShapeDtypeStruct((ROWS, WIDTH), jnp.float32),
            jax.ShapeDtypeStruct((ROWS, WIDTH), jnp.bfloat16),
            pltpu.VMEM((16, ROWS, WIDTH), jnp.bfloat16),
            jax.ShapeDtypeStruct((ROWS, WIDTH), jnp.float32),
            jax.ShapeDtypeStruct((8, WIDTH), jnp.float32),
        ),
        scratch_shapes=[
            pltpu.VMEM((ROWS, D_IN), jnp.bfloat16),
            pltpu.VMEM((D_IN, WIDTH), jnp.bfloat16),
            pltpu.VMEM((1, ROWS), jnp.int32),
            pltpu.SemaphoreType.DMA((PIECES,)),
            pltpu.SemaphoreType.DMA((PIECES,)),
            pltpu.SemaphoreType.DMA,
        ],
        compiler_params=params(8),
        name="project",
    )(hidden, weight, partner.reshape(1, ROWS))


def score_body(place_ref, rows_ref, columns_ref, pair_sum_ref, powers_ref, sums_ref, left, right):
    for b in range(16):
        shard = rows_ref[lax.rem(place_ref[0] + b, 16)]
        scaled = shard.astype(jnp.float32) * (inverse_tau * log2_e)
        high = scaled.astype(jnp.bfloat16)
        left[b * ROWS : (b + 1) * ROWS, :WIDTH] = high
        left[b * ROWS : (b + 1) * ROWS, WIDTH:] = (scaled - high.astype(jnp.float32)).astype(jnp.bfloat16)
    chunk = 2 * WIDTH
    for n in range(SPAN // chunk):
        columns = slice(n * chunk, (n + 1) * chunk)
        piece = jnp.transpose(columns_ref[columns, :])
        right[:WIDTH, columns] = piece
        right[WIDTH:, columns] = piece
    for n in range(SPAN // chunk):
        columns = slice(n * chunk, (n + 1) * chunk)
        powers = jnp.exp2(jnp.dot(left[...], right[:, columns], preferred_element_type=jnp.float32))
        own_row = lax.broadcasted_iota(jnp.int32, (ROWS, chunk), 0) + place_ref[1] * ROWS
        own_column = lax.broadcasted_iota(jnp.int32, (ROWS, chunk), 1) + n * chunk
        first = jnp.where(own_row == own_column, 0.0, powers[:ROWS, :])
        rest = powers[ROWS:, :]
        powers_ref[:ROWS, columns] = first.astype(jnp.bfloat16)
        powers_ref[ROWS:, columns] = rest.astype(jnp.bfloat16)
        sums = jnp.sum(first.reshape(ROWS // 8, 8, chunk), axis=0)
        sums += jnp.sum(rest.reshape((SPAN - ROWS) // 8, 8, chunk), axis=0)
        sums = jnp.sum(sums, axis=0, keepdims=True)
        for half in range(2):
            sums_ref[2 * n + half : 2 * n + half + 1, :] = sums[:, half * WIDTH : (half + 1) * WIDTH]
    sums_ref[TILES:, :] = pair_sum_ref[...]


def score(place, rows, columns, pair_sum):
    return pl.pallas_call(
        score_body,
        in_specs=[SMEM] + [VMEM] * 3,
        out_specs=(VMEM, VMEM),
        out_shape=(
            pltpu.VMEM((SPAN, SPAN), jnp.bfloat16),
            pltpu.VMEM((TILES + 8, WIDTH), jnp.float32),
        ),
        scratch_shapes=[
            pltpu.VMEM((SPAN, 2 * WIDTH), jnp.bfloat16),
            pltpu.VMEM((2 * WIDTH, SPAN), jnp.bfloat16),
        ],
        compiler_params=params(20),
        name="score",
    )(place, rows, columns, pair_sum)


def spread_body(arrived_ref, copies_ref):
    total = arrived_ref[: TILES + 8, :] + arrived_ref[TILES + 8 :, :]
    for k in range(8):
        copies_ref[k] = total


def spread(arrived):
    return pl.pallas_call(
        spread_body,
        in_specs=[VMEM],
        out_specs=VMEM,
        out_shape=pltpu.VMEM((8, TILES + 8, WIDTH), jnp.float32),
        compiler_params=params(4),
        name="spread",
    )(arrived)


def weigh_body(place_ref, partial_ref, columns_ref, powers_ref, out_ref, own_ref, loss_ref, inverse, both):
    sums = jnp.sum(partial_ref[...], axis=0)
    totals = sums[:TILES, :]
    loss_ref[...] = total_of(jnp.log(totals)) - sums[TILES:, :]
    inverses = 1.0 / totals
    for k in range(TILES):
        rows = slice(k * WIDTH, (k + 1) * WIDTH)
        turned = jnp.transpose(jnp.broadcast_to(inverses[k : k + 1, :], (WIDTH, WIDTH)))
        inverse[rows, :] = turned
        piece = columns_ref[rows, :]
        both[rows, :WIDTH] = piece
        both[rows, WIDTH:] = (piece.astype(jnp.float32) * turned).astype(jnp.bfloat16)
    own_ref[...] = inverse[pl.ds(pl.multiple_of(place_ref[1] * ROWS, ROWS), ROWS), :]
    block = 4 * ROWS
    for i in range(SPAN // block):
        weighed = jnp.dot(
            powers_ref[i * block : (i + 1) * block, :], both[...], preferred_element_type=jnp.float32
        ).astype(jnp.bfloat16)
        for b in range(4):
            out_ref[lax.rem(place_ref[0] + 4 * i + b, 16)] = weighed[b * ROWS : (b + 1) * ROWS, :]


def weigh(place, partial, columns, powers):
    return pl.pallas_call(
        weigh_body,
        in_specs=[SMEM] + [VMEM] * 3,
        out_specs=(VMEM,) * 3,
        out_shape=(
            pltpu.VMEM((16, ROWS, 2 * WIDTH), jnp.bfloat16),
            jax.ShapeDtypeStruct((ROWS, WIDTH), jnp.float32),
            jax.ShapeDtypeStruct((8, WIDTH), jnp.float32),
        ),
        scratch_shapes=[
            pltpu.VMEM((SPAN, WIDTH), jnp.float32),
            pltpu.VMEM((SPAN, 2 * WIDTH), jnp.bfloat16),
        ],
        compiler_params=params(20),
        name="weigh",
    )(place, partial, columns, powers)


def gradient_body(
    core_ref, arrived_ref, inverse_ref, pair_ref, projected_ref, hidden_ref, derivative_ref, own_ref, other_ref
):
    sums = jnp.sum(arrived_ref[...].astype(jnp.float32), axis=0)
    mixed = inverse_ref[...] * sums[:, :WIDTH] + sums[:, WIDTH:]
    derivative = inverse_tau * (mixed - 2.0 * pair_ref[...])
    derivative_ref[...] = derivative
    projected = projected_ref[...]
    inverse_norm = lax.rsqrt(jnp.sum(projected * projected, axis=1, keepdims=True) + norm_epsilon)
    unit = projected * inverse_norm
    alongside = jnp.sum(unit * derivative, axis=1, keepdims=True)
    projected_grad = ((derivative - unit * alongside) * inverse_norm).astype(jnp.bfloat16)

    def product(half):
        columns = pl.ds(pl.multiple_of(half * HALF, HALF), HALF)
        return lax.dot_general(
            hidden_ref[:, columns], projected_grad, (((0,), (0,)), ((), ())), preferred_element_type=jnp.float32
        )

    own_ref[...] = product(core_ref[0])
    other_ref[...] = product(1 - core_ref[0]).astype(jnp.bfloat16)


def gradient(core, arrived, inverse, pair, projected, hidden):
    return pl.pallas_call(
        gradient_body,
        in_specs=[SMEM] + [VMEM] * 5,
        out_specs=(VMEM,) * 3,
        out_shape=(
            jax.ShapeDtypeStruct((ROWS, WIDTH), jnp.float32),
            pltpu.VMEM((HALF, WIDTH), jnp.float32),
            pltpu.VMEM((HALF, WIDTH), jnp.bfloat16),
        ),
        compiler_params=params(16),
        name="gradient",
    )(core, arrived, inverse, pair, projected, hidden)


def join_body(own_ref, other_ref, sum_ref):
    for k in range(16):
        part = slice(k * SHARE, (k + 1) * SHARE)
        sum_ref[k] = (own_ref[part, :] + other_ref[part, :].astype(jnp.float32)).astype(jnp.bfloat16)


def join(own, other):
    return pl.pallas_call(
        join_body,
        in_specs=[VMEM] * 2,
        out_specs=VMEM,
        out_shape=pltpu.VMEM((16, SHARE, WIDTH), jnp.bfloat16),
        compiler_params=params(4),
        name="join",
    )(own, other)


def share_body(arrived_ref, copies_ref):
    total = jnp.sum(arrived_ref[...].astype(jnp.float32), axis=0).astype(jnp.bfloat16)
    for k in range(8):
        copies_ref[k] = total


def share(arrived):
    return pl.pallas_call(
        share_body,
        in_specs=[VMEM],
        out_specs=VMEM,
        out_shape=pltpu.VMEM((8, SHARE, WIDTH), jnp.bfloat16),
        compiler_params=params(4),
        name="share",
    )(arrived)


def packet_body(arrived_ref, loss_ref, copies_ref):
    total = jnp.sum(arrived_ref[...].astype(jnp.float32), axis=0).astype(jnp.bfloat16)
    loss = jnp.broadcast_to(loss_ref[0:1, :], (16, WIDTH))
    high = loss.astype(jnp.bfloat16).astype(jnp.float32)
    middle = (loss - high).astype(jnp.bfloat16).astype(jnp.float32)
    low = loss - high - middle
    row = lax.broadcasted_iota(jnp.int32, (16, WIDTH), 0)
    pieces = jnp.where(row == 0, high, jnp.where(row == 1, middle, jnp.where(row == 2, low, 0.0)))
    pieces = pieces.astype(jnp.bfloat16)
    for k in range(16):
        copies_ref[k, :SHARE, :] = total
        copies_ref[k, SHARE:, :] = pieces


def packet(arrived, loss):
    return pl.pallas_call(
        packet_body,
        in_specs=[VMEM] * 2,
        out_specs=VMEM,
        out_shape=pltpu.VMEM((16, SHARE + 16, WIDTH), jnp.bfloat16),
        compiler_params=params(8),
        name="packet",
    )(arrived, loss)


def finish_body(arrived_ref, loss_ref, grad_ref):
    for k in range(32):
        grad_ref[k] = arrived_ref[k, :SHARE, :].astype(jnp.float32)
    pieces = jnp.sum(arrived_ref[:, SHARE:, :].astype(jnp.float32), axis=0)
    loss_ref[...] = jnp.sum(pieces[:, 0:1], axis=0, keepdims=True) * (0.5 / (256 * ROWS))


def finish(arrived):
    return pl.pallas_call(
        finish_body,
        in_specs=[VMEM],
        out_specs=(VMEM, VMEM),
        out_shape=(
            jax.ShapeDtypeStruct((1, 1), jnp.float32),
            jax.ShapeDtypeStruct((32, SHARE, WIDTH), jnp.float32),
        ),
        compiler_params=params(8),
        name="finish",
    )(arrived)


def local(hidden, weight, partner):
    plane_place = (lax.axis_index("y") * 2 + lax.axis_index("xl")) * 2 + lax.axis_index("xh")
    column_place = lax.axis_index("z") * 2 + lax.axis_index("c")
    core = lax.axis_index("c").astype(jnp.int32).reshape(1)
    place = jnp.stack([plane_place, column_place]).astype(jnp.int32)

    projected, features, copies, pair, pair_sum = project(hidden, weight, partner)
    columns = lax.all_gather(features, COLUMN, axis=0, tiled=True)
    rows = lax.all_to_all(copies, PLANE, 0, 0)
    powers, sums = score(place, rows, columns, pair_sum)
    sums = spread(lax.all_gather(sums, "c", axis=0, tiled=True))
    partial = lax.all_to_all(sums, "z", 0, 0)
    weighed, inverse, loss = weigh(place, partial, columns, powers)
    arrived = lax.all_to_all(weighed, PLANE, 0, 0)
    derivative, own, other = gradient(core, arrived, inverse, pair, projected, hidden)
    other = lax.ppermute(other, "c", [(0, 1), (1, 0)])
    shares = lax.all_to_all(join(own, other), PLANE, 0, 0)
    shares = lax.all_to_all(share(shares), "z", 0, 0)
    packets = lax.all_to_all(packet(shares, loss), PLANE, 0, 0)
    packets = lax.all_gather(packets, "c", axis=0, tiled=True)
    mean_loss, grad_weight = finish(packets)
    return (mean_loss.reshape(()), derivative, grad_weight.reshape(D_IN, WIDTH))


def solution(mesh):
    split = Mesh(mesh.devices.reshape(4, 2, 2, 8, 2), AXES)
    return jax.shard_map(
        local,
        mesh=split,
        in_specs=(P(AXES, None), P(), P(AXES)),
        out_specs=(P(), P(AXES, None), P()),
        check_vma=False,
    )
```

```python
import jax
import jax.numpy as jnp
from jax import lax
from jax.experimental import pallas as pl
from jax.experimental.pallas import tpu as pltpu
from jax.sharding import Mesh
from jax.sharding import PartitionSpec as P

inverse_tau = 10.0
norm_epsilon = 1e-06
log2_e = 1.4426950408889634

AXES = ("y", "xl", "c", "z", "xh")
PLANE = ("y", "xl", "xh")
COLUMN = ("z", "c")
ROWS = 192
WIDTH = 128
D_IN = 2048
SPAN = 16 * ROWS
TILES = SPAN // WIDTH
SHARE = D_IN // 32
HALF = D_IN // 2
PIECES = 2
MEBI = 1024 * 1024

VMEM = pl.BlockSpec(memory_space=pltpu.VMEM)
SMEM = pl.BlockSpec(memory_space=pltpu.SMEM)
ANY = pl.BlockSpec(memory_space=pl.ANY)


def params(size):
    return pltpu.CompilerParams(vmem_limit_bytes=size * MEBI)


def total_of(values):
    return jnp.sum(jnp.sum(values, axis=1, keepdims=True), axis=0, keepdims=True)


def project_body(
    hidden_hbm, weight_hbm, partner_hbm, projected_ref, features_ref, copies_ref, pair_ref, pair_sum_ref,
    hidden, weight, partner, hidden_done, weight_done, partner_done,
):
    depth = D_IN // PIECES
    copies = []
    for k in range(PIECES):
        part = slice(k * depth, (k + 1) * depth)
        copies.append(
            (
                pltpu.make_async_copy(hidden_hbm.at[:, part], hidden.at[:, part], hidden_done.at[k]),
                pltpu.make_async_copy(weight_hbm.at[part, :], weight.at[part, :], weight_done.at[k]),
            )
        )
    partner_copy = pltpu.make_async_copy(partner_hbm, partner, partner_done)
    for first, second in copies:
        first.start()
        second.start()
    partner_copy.start()
    projected = jnp.zeros((ROWS, WIDTH), jnp.float32)
    for k in range(PIECES):
        part = slice(k * depth, (k + 1) * depth)
        for copy in copies[k]:
            copy.wait()
        projected += jnp.dot(hidden[:, part], weight[part, :], preferred_element_type=jnp.float32)
    inverse_norm = lax.rsqrt(jnp.sum(projected * projected, axis=1, keepdims=True) + norm_epsilon)
    features = (projected * inverse_norm).astype(jnp.bfloat16)
    features_ref[...] = features
    for k in range(16):
        copies_ref[k] = features
    partner_copy.wait()
    places = lax.rem(partner[...], ROWS)
    picks = lax.broadcasted_iota(jnp.int32, (ROWS, ROWS), 0) == places
    paired = jnp.dot(
        jnp.where(picks, 1.0, 0.0).astype(jnp.bfloat16), features, preferred_element_type=jnp.float32
    )
    projected_ref[...] = projected
    pair_ref[...] = paired
    total = total_of(features.astype(jnp.float32) * paired)
    pair_sum_ref[...] = jnp.broadcast_to(inverse_tau * total, (8, WIDTH))


def project(hidden, weight, partner):
    return pl.pallas_call(
        project_body,
        in_specs=[ANY] * 3,
        out_specs=(VMEM,) * 5,
        out_shape=(
            jax.ShapeDtypeStruct((ROWS, WIDTH), jnp.float32),
            jax.ShapeDtypeStruct((ROWS, WIDTH), jnp.bfloat16),
            pltpu.VMEM((16, ROWS, WIDTH), jnp.bfloat16),
            jax.ShapeDtypeStruct((ROWS, WIDTH), jnp.float32),
            jax.ShapeDtypeStruct((8, WIDTH), jnp.float32),
        ),
        scratch_shapes=[
            pltpu.VMEM((ROWS, D_IN), jnp.bfloat16),
            pltpu.VMEM((D_IN, WIDTH), jnp.bfloat16),
            pltpu.VMEM((1, ROWS), jnp.int32),
            pltpu.SemaphoreType.DMA((PIECES,)),
            pltpu.SemaphoreType.DMA((PIECES,)),
            pltpu.SemaphoreType.DMA,
        ],
        compiler_params=params(60),
        name="project",
    )(hidden, weight, partner.reshape(1, ROWS))


def score_body(place_ref, rows_ref, columns_ref, pair_sum_ref, powers_ref, sums_ref, left, right):
    for b in range(16):
        shard = rows_ref[lax.rem(place_ref[0] + b, 16)]
        scaled = shard.astype(jnp.float32) * (inverse_tau * log2_e)
        high = scaled.astype(jnp.bfloat16)
        left[b * ROWS : (b + 1) * ROWS, :WIDTH] = high
        left[b * ROWS : (b + 1) * ROWS, WIDTH:] = (scaled - high.astype(jnp.float32)).astype(jnp.bfloat16)
    chunk = 2 * WIDTH
    for n in range(SPAN // chunk):
        columns = slice(n * chunk, (n + 1) * chunk)
        piece = jnp.transpose(columns_ref[columns, :])
        right[:WIDTH, columns] = piece
        right[WIDTH:, columns] = piece
    for n in range(SPAN // chunk):
        columns = slice(n * chunk, (n + 1) * chunk)
        powers = jnp.exp2(jnp.dot(left[...], right[:, columns], preferred_element_type=jnp.float32))
        own_row = lax.broadcasted_iota(jnp.int32, (ROWS, chunk), 0) + place_ref[1] * ROWS
        own_column = lax.broadcasted_iota(jnp.int32, (ROWS, chunk), 1) + n * chunk
        first = jnp.where(own_row == own_column, 0.0, powers[:ROWS, :])
        rest = powers[ROWS:, :]
        powers_ref[:ROWS, columns] = first.astype(jnp.bfloat16)
        powers_ref[ROWS:, columns] = rest.astype(jnp.bfloat16)
        sums = jnp.sum(first.reshape(ROWS // 8, 8, chunk), axis=0)
        sums += jnp.sum(rest.reshape((SPAN - ROWS) // 8, 8, chunk), axis=0)
        sums = jnp.sum(sums, axis=0, keepdims=True)
        for half in range(2):
            sums_ref[2 * n + half : 2 * n + half + 1, :] = sums[:, half * WIDTH : (half + 1) * WIDTH]
    sums_ref[TILES:, :] = pair_sum_ref[...]


def score(place, rows, columns, pair_sum):
    return pl.pallas_call(
        score_body,
        in_specs=[SMEM] + [VMEM] * 3,
        out_specs=(VMEM, VMEM),
        out_shape=(
            pltpu.VMEM((SPAN, SPAN), jnp.bfloat16),
            pltpu.VMEM((TILES + 8, WIDTH), jnp.float32),
        ),
        scratch_shapes=[
            pltpu.VMEM((SPAN, 2 * WIDTH), jnp.bfloat16),
            pltpu.VMEM((2 * WIDTH, SPAN), jnp.bfloat16),
        ],
        compiler_params=params(20),
        name="score",
    )(place, rows, columns, pair_sum)


def spread_body(arrived_ref, copies_ref):
    total = arrived_ref[: TILES + 8, :] + arrived_ref[TILES + 8 :, :]
    for k in range(8):
        copies_ref[k] = total


def spread(arrived):
    return pl.pallas_call(
        spread_body,
        in_specs=[VMEM],
        out_specs=VMEM,
        out_shape=pltpu.VMEM((8, TILES + 8, WIDTH), jnp.float32),
        compiler_params=params(4),
        name="spread",
    )(arrived)


def weigh_body(place_ref, partial_ref, columns_ref, powers_ref, out_ref, own_ref, loss_ref, inverse, both):
    sums = jnp.sum(partial_ref[...], axis=0)
    totals = sums[:TILES, :]
    loss_ref[...] = total_of(jnp.log(totals)) - sums[TILES:, :]
    inverses = 1.0 / totals
    for k in range(TILES):
        rows = slice(k * WIDTH, (k + 1) * WIDTH)
        turned = jnp.transpose(jnp.broadcast_to(inverses[k : k + 1, :], (WIDTH, WIDTH)))
        inverse[rows, :] = turned
        piece = columns_ref[rows, :]
        both[rows, :WIDTH] = piece
        both[rows, WIDTH:] = (piece.astype(jnp.float32) * turned).astype(jnp.bfloat16)
    own_ref[...] = inverse[pl.ds(pl.multiple_of(place_ref[1] * ROWS, ROWS), ROWS), :]
    block = 4 * ROWS
    for i in range(SPAN // block):
        weighed = jnp.dot(
            powers_ref[i * block : (i + 1) * block, :], both[...], preferred_element_type=jnp.float32
        ).astype(jnp.bfloat16)
        for b in range(4):
            out_ref[lax.rem(place_ref[0] + 4 * i + b, 16)] = weighed[b * ROWS : (b + 1) * ROWS, :]


def weigh(place, partial, columns, powers):
    return pl.pallas_call(
        weigh_body,
        in_specs=[SMEM] + [VMEM] * 3,
        out_specs=(VMEM,) * 3,
        out_shape=(
            pltpu.VMEM((16, ROWS, 2 * WIDTH), jnp.bfloat16),
            jax.ShapeDtypeStruct((ROWS, WIDTH), jnp.float32),
            jax.ShapeDtypeStruct((8, WIDTH), jnp.float32),
        ),
        scratch_shapes=[
            pltpu.VMEM((SPAN, WIDTH), jnp.float32),
            pltpu.VMEM((SPAN, 2 * WIDTH), jnp.bfloat16),
        ],
        compiler_params=params(20),
        name="weigh",
    )(place, partial, columns, powers)


def gradient_body(
    core_ref, arrived_ref, inverse_ref, pair_ref, projected_ref, hidden_ref, derivative_ref, own_ref, other_ref
):
    sums = jnp.sum(arrived_ref[...].astype(jnp.float32), axis=0)
    mixed = inverse_ref[...] * sums[:, :WIDTH] + sums[:, WIDTH:]
    derivative = inverse_tau * (mixed - 2.0 * pair_ref[...])
    derivative_ref[...] = derivative
    projected = projected_ref[...]
    inverse_norm = lax.rsqrt(jnp.sum(projected * projected, axis=1, keepdims=True) + norm_epsilon)
    unit = projected * inverse_norm
    alongside = jnp.sum(unit * derivative, axis=1, keepdims=True)
    projected_grad = ((derivative - unit * alongside) * inverse_norm).astype(jnp.bfloat16)

    def product(half):
        columns = pl.ds(pl.multiple_of(half * HALF, HALF), HALF)
        return lax.dot_general(
            hidden_ref[:, columns], projected_grad, (((0,), (0,)), ((), ())), preferred_element_type=jnp.float32
        )

    own_ref[...] = product(core_ref[0])
    other_ref[...] = product(1 - core_ref[0]).astype(jnp.bfloat16)


def gradient(core, arrived, inverse, pair, projected, hidden):
    return pl.pallas_call(
        gradient_body,
        in_specs=[SMEM] + [VMEM] * 5,
        out_specs=(VMEM,) * 3,
        out_shape=(
            jax.ShapeDtypeStruct((ROWS, WIDTH), jnp.float32),
            pltpu.VMEM((HALF, WIDTH), jnp.float32),
            pltpu.VMEM((HALF, WIDTH), jnp.bfloat16),
        ),
        compiler_params=params(16),
        name="gradient",
    )(core, arrived, inverse, pair, projected, hidden)


def join_body(own_ref, other_ref, sum_ref):
    for k in range(16):
        part = slice(k * SHARE, (k + 1) * SHARE)
        sum_ref[k] = (own_ref[part, :] + other_ref[part, :].astype(jnp.float32)).astype(jnp.bfloat16)


def join(own, other):
    return pl.pallas_call(
        join_body,
        in_specs=[VMEM] * 2,
        out_specs=VMEM,
        out_shape=pltpu.VMEM((16, SHARE, WIDTH), jnp.bfloat16),
        compiler_params=params(4),
        name="join",
    )(own, other)


def share_body(arrived_ref, copies_ref):
    total = jnp.sum(arrived_ref[...].astype(jnp.float32), axis=0).astype(jnp.bfloat16)
    for k in range(8):
        copies_ref[k] = total


def share(arrived):
    return pl.pallas_call(
        share_body,
        in_specs=[VMEM],
        out_specs=VMEM,
        out_shape=pltpu.VMEM((8, SHARE, WIDTH), jnp.bfloat16),
        compiler_params=params(4),
        name="share",
    )(arrived)


def packet_body(arrived_ref, loss_ref, copies_ref):
    total = jnp.sum(arrived_ref[...].astype(jnp.float32), axis=0).astype(jnp.bfloat16)
    loss = jnp.broadcast_to(loss_ref[0:1, :], (16, WIDTH))
    high = loss.astype(jnp.bfloat16).astype(jnp.float32)
    middle = (loss - high).astype(jnp.bfloat16).astype(jnp.float32)
    low = loss - high - middle
    row = lax.broadcasted_iota(jnp.int32, (16, WIDTH), 0)
    pieces = jnp.where(row == 0, high, jnp.where(row == 1, middle, jnp.where(row == 2, low, 0.0)))
    pieces = pieces.astype(jnp.bfloat16)
    for k in range(16):
        copies_ref[k, :SHARE, :] = total
        copies_ref[k, SHARE:, :] = pieces


def packet(arrived, loss):
    return pl.pallas_call(
        packet_body,
        in_specs=[VMEM] * 2,
        out_specs=VMEM,
        out_shape=pltpu.VMEM((16, SHARE + 16, WIDTH), jnp.bfloat16),
        compiler_params=params(8),
        name="packet",
    )(arrived, loss)


def finish_body(arrived_ref, loss_ref, grad_ref):
    for k in range(32):
        grad_ref[k] = arrived_ref[k, :SHARE, :].astype(jnp.float32)
    pieces = jnp.sum(arrived_ref[:, SHARE:, :].astype(jnp.float32), axis=0)
    loss_ref[...] = jnp.sum(pieces[:, 0:1], axis=0, keepdims=True) * (0.5 / (256 * ROWS))


def finish(arrived):
    return pl.pallas_call(
        finish_body,
        in_specs=[VMEM],
        out_specs=(VMEM, VMEM),
        out_shape=(
            jax.ShapeDtypeStruct((1, 1), jnp.float32),
            jax.ShapeDtypeStruct((32, SHARE, WIDTH), jnp.float32),
        ),
        compiler_params=params(8),
        name="finish",
    )(arrived)


def local(hidden, weight, partner):
    plane_place = (lax.axis_index("y") * 2 + lax.axis_index("xl")) * 2 + lax.axis_index("xh")
    column_place = lax.axis_index("z") * 2 + lax.axis_index("c")
    core = lax.axis_index("c").astype(jnp.int32).reshape(1)
    place = jnp.stack([plane_place, column_place]).astype(jnp.int32)

    projected, features, copies, pair, pair_sum = project(hidden, weight, partner)
    columns = lax.all_gather(features, COLUMN, axis=0, tiled=True)
    rows = lax.all_to_all(copies, PLANE, 0, 0)
    powers, sums = score(place, rows, columns, pair_sum)
    sums = spread(lax.all_gather(sums, "c", axis=0, tiled=True))
    partial = lax.all_to_all(sums, "z", 0, 0)
    weighed, inverse, loss = weigh(place, partial, columns, powers)
    arrived = lax.all_to_all(weighed, PLANE, 0, 0)
    derivative, own, other = gradient(core, arrived, inverse, pair, projected, hidden)
    other = lax.ppermute(other, "c", [(0, 1), (1, 0)])
    shares = lax.all_to_all(join(own, other), PLANE, 0, 0)
    shares = lax.all_to_all(share(shares), "z", 0, 0)
    packets = lax.all_to_all(packet(shares, loss), PLANE, 0, 0)
    packets = lax.all_gather(packets, "c", axis=0, tiled=True)
    mean_loss, grad_weight = finish(packets)
    return (mean_loss.reshape(()), derivative, grad_weight.reshape(D_IN, WIDTH))


def solution(mesh):
    split = Mesh(mesh.devices.reshape(4, 2, 2, 8, 2), AXES)
    return jax.shard_map(
        local,
        mesh=split,
        in_specs=(P(AXES, None), P(), P(AXES)),
        out_specs=(P(), P(AXES, None), P()),
        check_vma=False,
    )
```

```python
import jax
import jax.numpy as jnp
from jax import lax
from jax.experimental import pallas as pl
from jax.experimental.pallas import tpu as pltpu
from jax.sharding import Mesh
from jax.sharding import PartitionSpec as P

inverse_tau = 10.0
norm_epsilon = 1e-06
log2_e = 1.4426950408889634

AXES = ("y", "xl", "c", "z", "xh")
PLANE = ("y", "xl", "xh")
COLUMN = ("z", "c")
ROWS = 192
WIDTH = 128
D_IN = 2048
SPAN = 16 * ROWS
TILES = SPAN // WIDTH
SHARE = D_IN // 32
HALF = D_IN // 2
PIECES = 2
MEBI = 1024 * 1024

VMEM = pl.BlockSpec(memory_space=pltpu.VMEM)
SMEM = pl.BlockSpec(memory_space=pltpu.SMEM)
HBM = pl.BlockSpec(memory_space=pltpu.HBM)


def params(size):
    return pltpu.CompilerParams(vmem_limit_bytes=size * MEBI)


def total_of(values):
    return jnp.sum(jnp.sum(values, axis=1, keepdims=True), axis=0, keepdims=True)


def project_body(
    hidden_hbm, weight_hbm, partner_hbm, projected_ref, features_ref, copies_ref, pair_ref, pair_sum_ref,
    hidden, weight, partner, hidden_done, weight_done, partner_done,
):
    depth = D_IN // PIECES
    copies = []
    for k in range(PIECES):
        part = slice(k * depth, (k + 1) * depth)
        copies.append(
            (
                pltpu.make_async_copy(hidden_hbm.at[:, part], hidden.at[:, part], hidden_done.at[k]),
                pltpu.make_async_copy(weight_hbm.at[part, :], weight.at[part, :], weight_done.at[k]),
            )
        )
    partner_copy = pltpu.make_async_copy(partner_hbm, partner, partner_done)
    for first, second in copies:
        first.start()
        second.start()
    partner_copy.start()
    projected = jnp.zeros((ROWS, WIDTH), jnp.float32)
    for k in range(PIECES):
        part = slice(k * depth, (k + 1) * depth)
        for copy in copies[k]:
            copy.wait()
        projected += jnp.dot(hidden[:, part], weight[part, :], preferred_element_type=jnp.float32)
    inverse_norm = lax.rsqrt(jnp.sum(projected * projected, axis=1, keepdims=True) + norm_epsilon)
    features = (projected * inverse_norm).astype(jnp.bfloat16)
    features_ref[...] = features
    for k in range(16):
        copies_ref[k] = features
    partner_copy.wait()
    places = lax.rem(partner[...], ROWS)
    picks = lax.broadcasted_iota(jnp.int32, (ROWS, ROWS), 0) == places
    paired = jnp.dot(
        jnp.where(picks, 1.0, 0.0).astype(jnp.bfloat16), features, preferred_element_type=jnp.float32
    )
    projected_ref[...] = projected
    pair_ref[...] = paired
    total = total_of(features.astype(jnp.float32) * paired)
    pair_sum_ref[...] = jnp.broadcast_to(inverse_tau * total, (8, WIDTH))


def project(hidden, weight, partner):
    return pl.pallas_call(
        project_body,
        in_specs=[HBM] * 3,
        out_specs=(VMEM,) * 5,
        out_shape=(
            jax.ShapeDtypeStruct((ROWS, WIDTH), jnp.float32),
            jax.ShapeDtypeStruct((ROWS, WIDTH), jnp.bfloat16),
            pltpu.VMEM((16, ROWS, WIDTH), jnp.bfloat16),
            jax.ShapeDtypeStruct((ROWS, WIDTH), jnp.float32),
            jax.ShapeDtypeStruct((8, WIDTH), jnp.float32),
        ),
        scratch_shapes=[
            pltpu.VMEM((ROWS, D_IN), jnp.bfloat16),
            pltpu.VMEM((D_IN, WIDTH), jnp.bfloat16),
            pltpu.VMEM((1, ROWS), jnp.int32),
            pltpu.SemaphoreType.DMA((PIECES,)),
            pltpu.SemaphoreType.DMA((PIECES,)),
            pltpu.SemaphoreType.DMA,
        ],
        compiler_params=params(60),
        name="project",
    )(hidden, weight, partner.reshape(1, ROWS))


def score_body(place_ref, rows_ref, columns_ref, pair_sum_ref, powers_ref, sums_ref, left, right):
    for b in range(16):
        shard = rows_ref[lax.rem(place_ref[0] + b, 16)]
        scaled = shard.astype(jnp.float32) * (inverse_tau * log2_e)
        high = scaled.astype(jnp.bfloat16)
        left[b * ROWS : (b + 1) * ROWS, :WIDTH] = high
        left[b * ROWS : (b + 1) * ROWS, WIDTH:] = (scaled - high.astype(jnp.float32)).astype(jnp.bfloat16)
    chunk = 2 * WIDTH
    for n in range(SPAN // chunk):
        columns = slice(n * chunk, (n + 1) * chunk)
        piece = jnp.transpose(columns_ref[columns, :])
        right[:WIDTH, columns] = piece
        right[WIDTH:, columns] = piece
    for n in range(SPAN // chunk):
        columns = slice(n * chunk, (n + 1) * chunk)
        powers = jnp.exp2(jnp.dot(left[...], right[:, columns], preferred_element_type=jnp.float32))
        own_row = lax.broadcasted_iota(jnp.int32, (ROWS, chunk), 0) + place_ref[1] * ROWS
        own_column = lax.broadcasted_iota(jnp.int32, (ROWS, chunk), 1) + n * chunk
        first = jnp.where(own_row == own_column, 0.0, powers[:ROWS, :])
        rest = powers[ROWS:, :]
        powers_ref[:ROWS, columns] = first.astype(jnp.bfloat16)
        powers_ref[ROWS:, columns] = rest.astype(jnp.bfloat16)
        sums = jnp.sum(first.reshape(ROWS // 8, 8, chunk), axis=0)
        sums += jnp.sum(rest.reshape((SPAN - ROWS) // 8, 8, chunk), axis=0)
        sums = jnp.sum(sums, axis=0, keepdims=True)
        for half in range(2):
            sums_ref[2 * n + half : 2 * n + half + 1, :] = sums[:, half * WIDTH : (half + 1) * WIDTH]
    sums_ref[TILES:, :] = pair_sum_ref[...]


def score(place, rows, columns, pair_sum):
    return pl.pallas_call(
        score_body,
        in_specs=[SMEM] + [VMEM] * 3,
        out_specs=(VMEM, VMEM),
        out_shape=(
            pltpu.VMEM((SPAN, SPAN), jnp.bfloat16),
            pltpu.VMEM((TILES + 8, WIDTH), jnp.float32),
        ),
        scratch_shapes=[
            pltpu.VMEM((SPAN, 2 * WIDTH), jnp.bfloat16),
            pltpu.VMEM((2 * WIDTH, SPAN), jnp.bfloat16),
        ],
        compiler_params=params(20),
        name="score",
    )(place, rows, columns, pair_sum)


def spread_body(arrived_ref, copies_ref):
    total = arrived_ref[: TILES + 8, :] + arrived_ref[TILES + 8 :, :]
    for k in range(8):
        copies_ref[k] = total


def spread(arrived):
    return pl.pallas_call(
        spread_body,
        in_specs=[VMEM],
        out_specs=VMEM,
        out_shape=pltpu.VMEM((8, TILES + 8, WIDTH), jnp.float32),
        compiler_params=params(4),
        name="spread",
    )(arrived)


def weigh_body(
    place_ref, partial_ref, columns_ref, powers_ref, out_hbm, own_ref, loss_ref, inverse, both, staged, sent
):
    sums = jnp.sum(partial_ref[...], axis=0)
    totals = sums[:TILES, :]
    loss_ref[...] = total_of(jnp.log(totals)) - sums[TILES:, :]
    inverses = 1.0 / totals
    for k in range(TILES):
        rows = slice(k * WIDTH, (k + 1) * WIDTH)
        turned = jnp.transpose(jnp.broadcast_to(inverses[k : k + 1, :], (WIDTH, WIDTH)))
        inverse[rows, :] = turned
        piece = columns_ref[rows, :]
        both[rows, :WIDTH] = piece
        both[rows, WIDTH:] = (piece.astype(jnp.float32) * turned).astype(jnp.bfloat16)
    own_ref[...] = inverse[pl.ds(pl.multiple_of(place_ref[1] * ROWS, ROWS), ROWS), :]
    block = 4 * ROWS
    copies = []
    for i in range(SPAN // block):
        weighed = jnp.dot(
            powers_ref[i * block : (i + 1) * block, :], both[...], preferred_element_type=jnp.float32
        ).astype(jnp.bfloat16)
        for b in range(4 * i, 4 * i + 4):
            staged[b] = weighed[(b - 4 * i) * ROWS : (b - 4 * i + 1) * ROWS, :]
            shard = lax.rem(place_ref[0] + b, 16)
            copies.append(pltpu.make_async_copy(staged.at[b], out_hbm.at[shard], sent.at[b]))
            copies[-1].start()
    for copy in copies:
        copy.wait()


def weigh(place, partial, columns, powers):
    return pl.pallas_call(
        weigh_body,
        in_specs=[SMEM] + [VMEM] * 3,
        out_specs=(HBM, VMEM, VMEM),
        out_shape=(
            pltpu.HBM((16, ROWS, 2 * WIDTH), jnp.bfloat16),
            jax.ShapeDtypeStruct((ROWS, WIDTH), jnp.float32),
            jax.ShapeDtypeStruct((8, WIDTH), jnp.float32),
        ),
        scratch_shapes=[
            pltpu.VMEM((SPAN, WIDTH), jnp.float32),
            pltpu.VMEM((SPAN, 2 * WIDTH), jnp.bfloat16),
            pltpu.VMEM((16, ROWS, 2 * WIDTH), jnp.bfloat16),
            pltpu.SemaphoreType.DMA((16,)),
        ],
        compiler_params=params(20),
        name="weigh",
    )(place, partial, columns, powers)


def gradient_body(
    core_ref, arrived_ref, inverse_ref, pair_ref, projected_ref, hidden_ref, derivative_ref, own_ref, other_ref
):
    sums = jnp.sum(arrived_ref[...].astype(jnp.float32), axis=0)
    mixed = inverse_ref[...] * sums[:, :WIDTH] + sums[:, WIDTH:]
    derivative = inverse_tau * (mixed - 2.0 * pair_ref[...])
    derivative_ref[...] = derivative
    projected = projected_ref[...]
    inverse_norm = lax.rsqrt(jnp.sum(projected * projected, axis=1, keepdims=True) + norm_epsilon)
    unit = projected * inverse_norm
    alongside = jnp.sum(unit * derivative, axis=1, keepdims=True)
    projected_grad = ((derivative - unit * alongside) * inverse_norm).astype(jnp.bfloat16)

    def product(half):
        columns = pl.ds(pl.multiple_of(half * HALF, HALF), HALF)
        return lax.dot_general(
            hidden_ref[:, columns], projected_grad, (((0,), (0,)), ((), ())), preferred_element_type=jnp.float32
        )

    own_ref[...] = product(core_ref[0])
    other_ref[...] = product(1 - core_ref[0]).astype(jnp.bfloat16)


def gradient(core, arrived, inverse, pair, projected, hidden):
    return pl.pallas_call(
        gradient_body,
        in_specs=[SMEM] + [VMEM] * 5,
        out_specs=(VMEM,) * 3,
        out_shape=(
            jax.ShapeDtypeStruct((ROWS, WIDTH), jnp.float32),
            pltpu.VMEM((HALF, WIDTH), jnp.float32),
            pltpu.VMEM((HALF, WIDTH), jnp.bfloat16),
        ),
        compiler_params=params(16),
        name="gradient",
    )(core, arrived, inverse, pair, projected, hidden)


def join_body(own_ref, other_ref, sum_ref):
    for k in range(16):
        part = slice(k * SHARE, (k + 1) * SHARE)
        sum_ref[k] = (own_ref[part, :] + other_ref[part, :].astype(jnp.float32)).astype(jnp.bfloat16)


def join(own, other):
    return pl.pallas_call(
        join_body,
        in_specs=[VMEM] * 2,
        out_specs=VMEM,
        out_shape=pltpu.VMEM((16, SHARE, WIDTH), jnp.bfloat16),
        compiler_params=params(4),
        name="join",
    )(own, other)


def share_body(arrived_ref, copies_ref):
    total = jnp.sum(arrived_ref[...].astype(jnp.float32), axis=0).astype(jnp.bfloat16)
    for k in range(8):
        copies_ref[k] = total


def share(arrived):
    return pl.pallas_call(
        share_body,
        in_specs=[VMEM],
        out_specs=VMEM,
        out_shape=pltpu.VMEM((8, SHARE, WIDTH), jnp.bfloat16),
        compiler_params=params(4),
        name="share",
    )(arrived)


def packet_body(arrived_ref, loss_ref, copies_ref):
    total = jnp.sum(arrived_ref[...].astype(jnp.float32), axis=0).astype(jnp.bfloat16)
    loss = jnp.broadcast_to(loss_ref[0:1, :], (16, WIDTH))
    high = loss.astype(jnp.bfloat16).astype(jnp.float32)
    middle = (loss - high).astype(jnp.bfloat16).astype(jnp.float32)
    low = loss - high - middle
    row = lax.broadcasted_iota(jnp.int32, (16, WIDTH), 0)
    pieces = jnp.where(row == 0, high, jnp.where(row == 1, middle, jnp.where(row == 2, low, 0.0)))
    pieces = pieces.astype(jnp.bfloat16)
    for k in range(16):
        copies_ref[k, :SHARE, :] = total
        copies_ref[k, SHARE:, :] = pieces


def packet(arrived, loss):
    return pl.pallas_call(
        packet_body,
        in_specs=[VMEM] * 2,
        out_specs=VMEM,
        out_shape=pltpu.VMEM((16, SHARE + 16, WIDTH), jnp.bfloat16),
        compiler_params=params(8),
        name="packet",
    )(arrived, loss)


def finish_body(arrived_ref, loss_ref, grad_ref):
    for k in range(32):
        grad_ref[k] = arrived_ref[k, :SHARE, :].astype(jnp.float32)
    pieces = jnp.sum(arrived_ref[:, SHARE:, :].astype(jnp.float32), axis=0)
    loss_ref[...] = jnp.sum(pieces[:, 0:1], axis=0, keepdims=True) * (0.5 / (256 * ROWS))


def finish(arrived):
    return pl.pallas_call(
        finish_body,
        in_specs=[VMEM],
        out_specs=(VMEM, VMEM),
        out_shape=(
            jax.ShapeDtypeStruct((1, 1), jnp.float32),
            jax.ShapeDtypeStruct((32, SHARE, WIDTH), jnp.float32),
        ),
        compiler_params=params(8),
        name="finish",
    )(arrived)


def local(hidden, weight, partner):
    plane_place = (lax.axis_index("y") * 2 + lax.axis_index("xl")) * 2 + lax.axis_index("xh")
    column_place = lax.axis_index("z") * 2 + lax.axis_index("c")
    core = lax.axis_index("c").astype(jnp.int32).reshape(1)
    place = jnp.stack([plane_place, column_place]).astype(jnp.int32)

    projected, features, copies, pair, pair_sum = project(hidden, weight, partner)
    columns = lax.all_gather(features, COLUMN, axis=0, tiled=True)
    rows = lax.all_to_all(copies, PLANE, 0, 0)
    powers, sums = score(place, rows, columns, pair_sum)
    sums = spread(lax.all_gather(sums, "c", axis=0, tiled=True))
    partial = lax.all_to_all(sums, "z", 0, 0)
    weighed, inverse, loss = weigh(place, partial, columns, powers)
    arrived = lax.all_to_all(weighed, PLANE, 0, 0)
    derivative, own, other = gradient(core, arrived, inverse, pair, projected, hidden)
    other = lax.ppermute(other, "c", [(0, 1), (1, 0)])
    shares = lax.all_to_all(join(own, other), PLANE, 0, 0)
    shares = lax.all_to_all(share(shares), "z", 0, 0)
    packets = lax.all_to_all(packet(shares, loss), PLANE, 0, 0)
    packets = lax.all_gather(packets, "c", axis=0, tiled=True)
    mean_loss, grad_weight = finish(packets)
    return (mean_loss.reshape(()), derivative, grad_weight.reshape(D_IN, WIDTH))


def solution(mesh):
    split = Mesh(mesh.devices.reshape(4, 2, 2, 8, 2), AXES)
    return jax.shard_map(
        local,
        mesh=split,
        in_specs=(P(AXES, None), P(), P(AXES)),
        out_specs=(P(), P(AXES, None), P()),
        check_vma=False,
    )
```

```python
import jax
import jax.numpy as jnp
from jax import lax
from jax.experimental import pallas as pl
from jax.experimental.pallas import tpu as pltpu
from jax.sharding import Mesh
from jax.sharding import PartitionSpec as P

inverse_tau = 10.0
norm_epsilon = 1e-06
log2_e = 1.4426950408889634

AXES = ("y", "xl", "c", "zh", "zm", "zl", "xh")
PLANE = ("y", "xl", "xh")
COLUMN = ("zh", "zm", "zl", "c")
DEPTH = ("zl", "zm", "zh")
ROWS = 192
WIDTH = 128
D_IN = 2048
SPAN = 16 * ROWS
TILES = SPAN // WIDTH
SHARE = D_IN // 32
HALF = D_IN // 2
PIECES = 4
MEBI = 1024 * 1024

VMEM = pl.BlockSpec(memory_space=pltpu.VMEM)
SMEM = pl.BlockSpec(memory_space=pltpu.SMEM)
HBM = pl.BlockSpec(memory_space=pltpu.HBM)


def params(size):
    return pltpu.CompilerParams(vmem_limit_bytes=size * MEBI)


def total_of(values):
    return jnp.sum(jnp.sum(values, axis=1, keepdims=True), axis=0, keepdims=True)


def project_body(
    hidden_hbm, weight_hbm, partner_hbm, projected_ref, features_ref, copies_hbm, pair_ref, pair_sum_ref,
    hidden, weight, partner, staged, hidden_done, weight_done, partner_done, sent,
):
    depth = D_IN // PIECES
    copies = []
    for k in range(PIECES):
        part = slice(k * depth, (k + 1) * depth)
        copies.append(
            (
                pltpu.make_async_copy(hidden_hbm.at[:, part], hidden.at[:, part], hidden_done.at[k]),
                pltpu.make_async_copy(weight_hbm.at[part, :], weight.at[part, :], weight_done.at[k]),
            )
        )
    partner_copy = pltpu.make_async_copy(partner_hbm, partner, partner_done)
    for first, second in copies:
        first.start()
        second.start()
    partner_copy.start()
    projected = jnp.zeros((ROWS, WIDTH), jnp.float32)
    for k in range(PIECES):
        part = slice(k * depth, (k + 1) * depth)
        for copy in copies[k]:
            copy.wait()
        projected += jnp.dot(hidden[:, part], weight[part, :], preferred_element_type=jnp.float32)
    inverse_norm = lax.rsqrt(jnp.sum(projected * projected, axis=1, keepdims=True) + norm_epsilon)
    features = (projected * inverse_norm).astype(jnp.bfloat16)
    staged[...] = features
    sends = [pltpu.make_async_copy(staged, copies_hbm.at[k], sent.at[k]) for k in range(16)]
    for send in sends:
        send.start()
    features_ref[...] = features
    partner_copy.wait()
    places = lax.rem(partner[...], ROWS)
    picks = lax.broadcasted_iota(jnp.int32, (ROWS, ROWS), 0) == places
    paired = jnp.dot(
        jnp.where(picks, 1.0, 0.0).astype(jnp.bfloat16), features, preferred_element_type=jnp.float32
    )
    projected_ref[...] = projected
    pair_ref[...] = paired
    total = total_of(features.astype(jnp.float32) * paired)
    pair_sum_ref[...] = jnp.broadcast_to(inverse_tau * total, (8, WIDTH))
    for send in sends:
        send.wait()


def project(hidden, weight, partner):
    return pl.pallas_call(
        project_body,
        in_specs=[HBM] * 3,
        out_specs=(VMEM, VMEM, HBM, VMEM, VMEM),
        out_shape=(
            jax.ShapeDtypeStruct((ROWS, WIDTH), jnp.float32),
            jax.ShapeDtypeStruct((ROWS, WIDTH), jnp.bfloat16),
            pltpu.HBM((16, ROWS, WIDTH), jnp.bfloat16),
            jax.ShapeDtypeStruct((ROWS, WIDTH), jnp.float32),
            jax.ShapeDtypeStruct((8, WIDTH), jnp.float32),
        ),
        scratch_shapes=[
            pltpu.VMEM((ROWS, D_IN), jnp.bfloat16),
            pltpu.VMEM((D_IN, WIDTH), jnp.bfloat16),
            pltpu.VMEM((1, ROWS), jnp.int32),
            pltpu.VMEM((ROWS, WIDTH), jnp.bfloat16),
            pltpu.SemaphoreType.DMA((PIECES,)),
            pltpu.SemaphoreType.DMA((PIECES,)),
            pltpu.SemaphoreType.DMA,
            pltpu.SemaphoreType.DMA((16,)),
        ],
        compiler_params=params(60),
        name="project",
    )(hidden, weight, partner.reshape(1, ROWS))


def score_body(place_ref, rows_ref, columns_ref, pair_sum_ref, powers_ref, sums_ref, left, right):
    for b in range(16):
        shard = rows_ref[lax.rem(place_ref[0] + b, 16)]
        scaled = shard.astype(jnp.float32) * (inverse_tau * log2_e)
        high = scaled.astype(jnp.bfloat16)
        left[b * ROWS : (b + 1) * ROWS, :WIDTH] = high
        left[b * ROWS : (b + 1) * ROWS, WIDTH:] = (scaled - high.astype(jnp.float32)).astype(jnp.bfloat16)
    chunk = 2 * WIDTH
    for n in range(SPAN // chunk):
        columns = slice(n * chunk, (n + 1) * chunk)
        piece = jnp.transpose(columns_ref[columns, :])
        right[:WIDTH, columns] = piece
        right[WIDTH:, columns] = piece
    for n in range(SPAN // chunk):
        columns = slice(n * chunk, (n + 1) * chunk)
        powers = jnp.exp2(jnp.dot(left[...], right[:, columns], preferred_element_type=jnp.float32))
        own_row = lax.broadcasted_iota(jnp.int32, (ROWS, chunk), 0) + place_ref[1] * ROWS
        own_column = lax.broadcasted_iota(jnp.int32, (ROWS, chunk), 1) + n * chunk
        first = jnp.where(own_row == own_column, 0.0, powers[:ROWS, :])
        rest = powers[ROWS:, :]
        powers_ref[:ROWS, columns] = first.astype(jnp.bfloat16)
        powers_ref[ROWS:, columns] = rest.astype(jnp.bfloat16)
        sums = jnp.sum(first.reshape(ROWS // 8, 8, chunk), axis=0)
        sums += jnp.sum(rest.reshape((SPAN - ROWS) // 8, 8, chunk), axis=0)
        sums = jnp.sum(sums, axis=0, keepdims=True)
        for half in range(2):
            sums_ref[2 * n + half : 2 * n + half + 1, :] = sums[:, half * WIDTH : (half + 1) * WIDTH]
    sums_ref[TILES:, :] = pair_sum_ref[...]


def score(place, rows, columns, pair_sum):
    return pl.pallas_call(
        score_body,
        in_specs=[SMEM] + [VMEM] * 3,
        out_specs=(VMEM, VMEM),
        out_shape=(
            pltpu.VMEM((SPAN, SPAN), jnp.bfloat16),
            pltpu.VMEM((TILES + 8, WIDTH), jnp.float32),
        ),
        scratch_shapes=[
            pltpu.VMEM((SPAN, 2 * WIDTH), jnp.bfloat16),
            pltpu.VMEM((2 * WIDTH, SPAN), jnp.bfloat16),
        ],
        compiler_params=params(20),
        name="score",
    )(place, rows, columns, pair_sum)


def spread_body(arrived_ref, copies_ref):
    total = arrived_ref[: TILES + 8, :] + arrived_ref[TILES + 8 :, :]
    for k in range(8):
        copies_ref[k] = total


def spread(arrived):
    return pl.pallas_call(
        spread_body,
        in_specs=[VMEM],
        out_specs=VMEM,
        out_shape=pltpu.VMEM((8, TILES + 8, WIDTH), jnp.float32),
        compiler_params=params(4),
        name="spread",
    )(arrived)


def weigh_body(place_ref, partial_ref, columns_ref, powers_ref, out_ref, own_ref, loss_ref, inverse, both):
    sums = jnp.sum(partial_ref[...], axis=0)
    totals = sums[:TILES, :]
    loss_ref[...] = total_of(jnp.log(totals)) - sums[TILES:, :]
    inverses = 1.0 / totals
    for k in range(TILES):
        rows = slice(k * WIDTH, (k + 1) * WIDTH)
        turned = jnp.transpose(jnp.broadcast_to(inverses[k : k + 1, :], (WIDTH, WIDTH)))
        inverse[rows, :] = turned
        piece = columns_ref[rows, :]
        both[rows, :WIDTH] = piece
        both[rows, WIDTH:] = (piece.astype(jnp.float32) * turned).astype(jnp.bfloat16)
    own_ref[...] = inverse[pl.ds(pl.multiple_of(place_ref[1] * ROWS, ROWS), ROWS), :]
    block = 4 * ROWS
    for i in range(SPAN // block):
        weighed = jnp.dot(
            powers_ref[i * block : (i + 1) * block, :], both[...], preferred_element_type=jnp.float32
        ).astype(jnp.bfloat16)
        for b in range(4):
            out_ref[lax.rem(place_ref[0] + 4 * i + b, 16)] = weighed[b * ROWS : (b + 1) * ROWS, :]


def weigh(place, partial, columns, powers):
    return pl.pallas_call(
        weigh_body,
        in_specs=[SMEM] + [VMEM] * 3,
        out_specs=(VMEM,) * 3,
        out_shape=(
            pltpu.VMEM((16, ROWS, 2 * WIDTH), jnp.bfloat16),
            jax.ShapeDtypeStruct((ROWS, WIDTH), jnp.float32),
            jax.ShapeDtypeStruct((8, WIDTH), jnp.float32),
        ),
        scratch_shapes=[
            pltpu.VMEM((SPAN, WIDTH), jnp.float32),
            pltpu.VMEM((SPAN, 2 * WIDTH), jnp.bfloat16),
        ],
        compiler_params=params(20),
        name="weigh",
    )(place, partial, columns, powers)


def gradient_body(
    core_ref, arrived_ref, inverse_ref, pair_ref, projected_ref, hidden_ref, derivative_ref, own_ref, other_ref
):
    sums = jnp.sum(arrived_ref[...].astype(jnp.float32), axis=0)
    mixed = inverse_ref[...] * sums[:, :WIDTH] + sums[:, WIDTH:]
    derivative = inverse_tau * (mixed - 2.0 * pair_ref[...])
    derivative_ref[...] = derivative
    projected = projected_ref[...]
    inverse_norm = lax.rsqrt(jnp.sum(projected * projected, axis=1, keepdims=True) + norm_epsilon)
    unit = projected * inverse_norm
    alongside = jnp.sum(unit * derivative, axis=1, keepdims=True)
    projected_grad = ((derivative - unit * alongside) * inverse_norm).astype(jnp.bfloat16)

    def product(half):
        columns = pl.ds(pl.multiple_of(half * HALF, HALF), HALF)
        return lax.dot_general(
            hidden_ref[:, columns], projected_grad, (((0,), (0,)), ((), ())), preferred_element_type=jnp.float32
        )

    own_ref[...] = product(core_ref[0])
    other_ref[...] = product(1 - core_ref[0]).astype(jnp.bfloat16)


def gradient(core, arrived, inverse, pair, projected, hidden):
    return pl.pallas_call(
        gradient_body,
        in_specs=[SMEM] + [VMEM] * 5,
        out_specs=(VMEM,) * 3,
        out_shape=(
            pltpu.VMEM((ROWS, WIDTH), jnp.float32),
            pltpu.VMEM((HALF, WIDTH), jnp.float32),
            pltpu.VMEM((HALF, WIDTH), jnp.bfloat16),
        ),
        compiler_params=params(16),
        name="gradient",
    )(core, arrived, inverse, pair, projected, hidden)


def join_body(own_ref, other_ref, sum_ref):
    for k in range(16):
        part = slice(k * SHARE, (k + 1) * SHARE)
        sum_ref[k] = (own_ref[part, :] + other_ref[part, :].astype(jnp.float32)).astype(jnp.bfloat16)


def join(own, other):
    return pl.pallas_call(
        join_body,
        in_specs=[VMEM] * 2,
        out_specs=VMEM,
        out_shape=pltpu.VMEM((16, SHARE, WIDTH), jnp.bfloat16),
        compiler_params=params(4),
        name="join",
    )(own, other)


def share_body(arrived_ref, copies_ref):
    total = jnp.sum(arrived_ref[...].astype(jnp.float32), axis=0).astype(jnp.bfloat16)
    for k in range(8):
        copies_ref[k] = total


def share(arrived):
    return pl.pallas_call(
        share_body,
        in_specs=[VMEM],
        out_specs=VMEM,
        out_shape=pltpu.VMEM((8, SHARE, WIDTH), jnp.bfloat16),
        compiler_params=params(4),
        name="share",
    )(arrived)


def packet_body(arrived_ref, loss_ref, copies_ref):
    total = jnp.sum(arrived_ref[...].astype(jnp.float32), axis=0).astype(jnp.bfloat16)
    loss = jnp.broadcast_to(loss_ref[0:1, :], (16, WIDTH))
    high = loss.astype(jnp.bfloat16).astype(jnp.float32)
    middle = (loss - high).astype(jnp.bfloat16).astype(jnp.float32)
    low = loss - high - middle
    row = lax.broadcasted_iota(jnp.int32, (16, WIDTH), 0)
    pieces = jnp.where(row == 0, high, jnp.where(row == 1, middle, jnp.where(row == 2, low, 0.0)))
    pieces = pieces.astype(jnp.bfloat16)
    for k in range(16):
        copies_ref[k, :SHARE, :] = total
        copies_ref[k, SHARE:, :] = pieces


def packet(arrived, loss):
    return pl.pallas_call(
        packet_body,
        in_specs=[VMEM] * 2,
        out_specs=VMEM,
        out_shape=pltpu.VMEM((16, SHARE + 16, WIDTH), jnp.bfloat16),
        compiler_params=params(8),
        name="packet",
    )(arrived, loss)


def finish_body(arrived_ref, loss_ref, grad_ref):
    for k in range(32):
        grad_ref[k] = arrived_ref[k, :SHARE, :].astype(jnp.float32)
    pieces = jnp.sum(arrived_ref[:, SHARE:, :].astype(jnp.float32), axis=0)
    loss_ref[...] = jnp.sum(pieces[:, 0:1], axis=0, keepdims=True) * (0.5 / (256 * ROWS))


def finish(arrived):
    return pl.pallas_call(
        finish_body,
        in_specs=[VMEM],
        out_specs=(VMEM, VMEM),
        out_shape=(
            jax.ShapeDtypeStruct((1, 1), jnp.float32),
            jax.ShapeDtypeStruct((32, SHARE, WIDTH), jnp.float32),
        ),
        compiler_params=params(8),
        name="finish",
    )(arrived)


def local(hidden, weight, partner):
    plane_place = (lax.axis_index("y") * 2 + lax.axis_index("xl")) * 2 + lax.axis_index("xh")
    deep_place = (lax.axis_index("zh") * 2 + lax.axis_index("zm")) * 2 + lax.axis_index("zl")
    column_place = deep_place * 2 + lax.axis_index("c")
    core = lax.axis_index("c").astype(jnp.int32).reshape(1)
    place = jnp.stack([plane_place, column_place]).astype(jnp.int32)

    projected, features, copies, pair, pair_sum = project(hidden, weight, partner)
    columns = lax.all_gather(features, COLUMN, axis=0, tiled=True)
    rows = lax.all_to_all(copies, PLANE, 0, 0)
    powers, sums = score(place, rows, columns, pair_sum)
    sums = spread(lax.all_gather(sums, "c", axis=0, tiled=True))
    partial = lax.all_to_all(sums, DEPTH, 0, 0)
    weighed, inverse, loss = weigh(place, partial, columns, powers)
    arrived = lax.all_to_all(weighed, PLANE, 0, 0)
    derivative, own, other = gradient(core, arrived, inverse, pair, projected, hidden)
    other = lax.ppermute(other, "c", [(0, 1), (1, 0)])
    shares = lax.all_to_all(join(own, other), PLANE, 0, 0)
    shares = lax.all_to_all(share(shares), DEPTH, 0, 0)
    packets = lax.all_to_all(packet(shares, loss), PLANE, 0, 0)
    packets = lax.all_gather(packets, "c", axis=0, tiled=True)
    mean_loss, grad_weight = finish(packets)
    return (mean_loss.reshape(()), derivative, grad_weight.reshape(D_IN, WIDTH))


def solution(mesh):
    split = Mesh(mesh.devices.reshape(4, 2, 2, 2, 2, 2, 2), AXES)
    return jax.shard_map(
        local,
        mesh=split,
        in_specs=(P(AXES, None), P(), P(AXES)),
        out_specs=(P(), P(AXES, None), P()),
        check_vma=False,
    )
```

```python
import jax
import jax.numpy as jnp
from jax import lax
from jax.experimental import pallas as pl
from jax.experimental.pallas import tpu as pltpu
from jax.sharding import Mesh
from jax.sharding import PartitionSpec as P

inverse_tau = 10.0
norm_epsilon = 1e-06
log2_e = 1.4426950408889634

AXES = ("y", "xl", "c", "z", "xh")
PLANE = ("xl", "xh", "y")
COLUMN = ("z", "c")
ROWS = 192
WIDTH = 128
D_IN = 2048
SPAN = 16 * ROWS
TILES = SPAN // WIDTH
SHARE = D_IN // 32
HALF = D_IN // 2
PIECES = 2
MEBI = 1024 * 1024

VMEM = pl.BlockSpec(memory_space=pltpu.VMEM)
SMEM = pl.BlockSpec(memory_space=pltpu.SMEM)
ANY = pl.BlockSpec(memory_space=pl.ANY)


def params(size):
    return pltpu.CompilerParams(vmem_limit_bytes=size * MEBI)


def total_of(values):
    return jnp.sum(jnp.sum(values, axis=1, keepdims=True), axis=0, keepdims=True)


def project_body(
    hidden_hbm, weight_hbm, partner_hbm, projected_ref, features_ref, copies_ref, pair_ref, pair_sum_ref,
    hidden, weight, partner, hidden_done, weight_done, partner_done,
):
    depth = D_IN // PIECES
    copies = []
    for k in range(PIECES):
        part = slice(k * depth, (k + 1) * depth)
        copies.append(
            (
                pltpu.make_async_copy(hidden_hbm.at[:, part], hidden.at[:, part], hidden_done.at[k]),
                pltpu.make_async_copy(weight_hbm.at[part, :], weight.at[part, :], weight_done.at[k]),
            )
        )
    partner_copy = pltpu.make_async_copy(partner_hbm, partner, partner_done)
    for first, second in copies:
        first.start()
        second.start()
    partner_copy.start()
    projected = jnp.zeros((ROWS, WIDTH), jnp.float32)
    for k in range(PIECES):
        part = slice(k * depth, (k + 1) * depth)
        for copy in copies[k]:
            copy.wait()
        projected += jnp.dot(hidden[:, part], weight[part, :], preferred_element_type=jnp.float32)
    inverse_norm = lax.rsqrt(jnp.sum(projected * projected, axis=1, keepdims=True) + norm_epsilon)
    features = (projected * inverse_norm).astype(jnp.bfloat16)
    features_ref[...] = features
    for k in range(16):
        copies_ref[k] = features
    partner_copy.wait()
    places = lax.rem(partner[...], ROWS)
    picks = lax.broadcasted_iota(jnp.int32, (ROWS, ROWS), 0) == places
    paired = jnp.dot(
        jnp.where(picks, 1.0, 0.0).astype(jnp.bfloat16), features, preferred_element_type=jnp.float32
    )
    projected_ref[...] = projected
    pair_ref[...] = paired
    total = total_of(features.astype(jnp.float32) * paired)
    pair_sum_ref[...] = jnp.broadcast_to(inverse_tau * total, (8, WIDTH))


def project(hidden, weight, partner):
    return pl.pallas_call(
        project_body,
        in_specs=[ANY] * 3,
        out_specs=(VMEM,) * 5,
        out_shape=(
            jax.ShapeDtypeStruct((ROWS, WIDTH), jnp.float32),
            jax.ShapeDtypeStruct((ROWS, WIDTH), jnp.bfloat16),
            pltpu.VMEM((16, ROWS, WIDTH), jnp.bfloat16),
            jax.ShapeDtypeStruct((ROWS, WIDTH), jnp.float32),
            jax.ShapeDtypeStruct((8, WIDTH), jnp.float32),
        ),
        scratch_shapes=[
            pltpu.VMEM((ROWS, D_IN), jnp.bfloat16),
            pltpu.VMEM((D_IN, WIDTH), jnp.bfloat16),
            pltpu.VMEM((1, ROWS), jnp.int32),
            pltpu.SemaphoreType.DMA((PIECES,)),
            pltpu.SemaphoreType.DMA((PIECES,)),
            pltpu.SemaphoreType.DMA,
        ],
        compiler_params=params(60),
        name="project",
    )(hidden, weight, partner.reshape(1, ROWS))


def score_body(place_ref, rows_ref, columns_ref, pair_sum_ref, powers_ref, sums_ref, left, right):
    for b in range(16):
        shard = rows_ref[lax.rem(place_ref[0] + b, 16)]
        scaled = shard.astype(jnp.float32) * (inverse_tau * log2_e)
        high = scaled.astype(jnp.bfloat16)
        left[b * ROWS : (b + 1) * ROWS, :WIDTH] = high
        left[b * ROWS : (b + 1) * ROWS, WIDTH:] = (scaled - high.astype(jnp.float32)).astype(jnp.bfloat16)
    chunk = 2 * WIDTH
    for n in range(SPAN // chunk):
        columns = slice(n * chunk, (n + 1) * chunk)
        piece = jnp.transpose(columns_ref[columns, :])
        right[:WIDTH, columns] = piece
        right[WIDTH:, columns] = piece
    for n in range(SPAN // chunk):
        columns = slice(n * chunk, (n + 1) * chunk)
        powers = jnp.exp2(jnp.dot(left[...], right[:, columns], preferred_element_type=jnp.float32))
        own_row = lax.broadcasted_iota(jnp.int32, (ROWS, chunk), 0) + place_ref[1] * ROWS
        own_column = lax.broadcasted_iota(jnp.int32, (ROWS, chunk), 1) + n * chunk
        first = jnp.where(own_row == own_column, 0.0, powers[:ROWS, :])
        rest = powers[ROWS:, :]
        powers_ref[:ROWS, columns] = first.astype(jnp.bfloat16)
        powers_ref[ROWS:, columns] = rest.astype(jnp.bfloat16)
        sums = jnp.sum(first.reshape(ROWS // 8, 8, chunk), axis=0)
        sums += jnp.sum(rest.reshape((SPAN - ROWS) // 8, 8, chunk), axis=0)
        sums = jnp.sum(sums, axis=0, keepdims=True)
        for half in range(2):
            sums_ref[2 * n + half : 2 * n + half + 1, :] = sums[:, half * WIDTH : (half + 1) * WIDTH]
    sums_ref[TILES:, :] = pair_sum_ref[...]


def score(place, rows, columns, pair_sum):
    return pl.pallas_call(
        score_body,
        in_specs=[SMEM] + [VMEM] * 3,
        out_specs=(VMEM, VMEM),
        out_shape=(
            pltpu.VMEM((SPAN, SPAN), jnp.bfloat16),
            pltpu.VMEM((TILES + 8, WIDTH), jnp.float32),
        ),
        scratch_shapes=[
            pltpu.VMEM((SPAN, 2 * WIDTH), jnp.bfloat16),
            pltpu.VMEM((2 * WIDTH, SPAN), jnp.bfloat16),
        ],
        compiler_params=params(20),
        name="score",
    )(place, rows, columns, pair_sum)


def spread_body(arrived_ref, copies_ref):
    total = arrived_ref[: TILES + 8, :] + arrived_ref[TILES + 8 :, :]
    for k in range(8):
        copies_ref[k] = total


def spread(arrived):
    return pl.pallas_call(
        spread_body,
        in_specs=[VMEM],
        out_specs=VMEM,
        out_shape=pltpu.VMEM((8, TILES + 8, WIDTH), jnp.float32),
        compiler_params=params(4),
        name="spread",
    )(arrived)


def weigh_body(place_ref, partial_ref, columns_ref, powers_ref, out_ref, own_ref, loss_ref, inverse, both):
    sums = jnp.sum(partial_ref[...], axis=0)
    totals = sums[:TILES, :]
    loss_ref[...] = total_of(jnp.log(totals)) - sums[TILES:, :]
    inverses = 1.0 / totals
    for k in range(TILES):
        rows = slice(k * WIDTH, (k + 1) * WIDTH)
        turned = jnp.transpose(jnp.broadcast_to(inverses[k : k + 1, :], (WIDTH, WIDTH)))
        inverse[rows, :] = turned
        piece = columns_ref[rows, :]
        both[rows, :WIDTH] = piece
        both[rows, WIDTH:] = (piece.astype(jnp.float32) * turned).astype(jnp.bfloat16)
    own_ref[...] = inverse[pl.ds(pl.multiple_of(place_ref[1] * ROWS, ROWS), ROWS), :]
    block = 4 * ROWS
    for i in range(SPAN // block):
        weighed = jnp.dot(
            powers_ref[i * block : (i + 1) * block, :], both[...], preferred_element_type=jnp.float32
        ).astype(jnp.bfloat16)
        for b in range(4):
            out_ref[lax.rem(place_ref[0] + 4 * i + b, 16)] = weighed[b * ROWS : (b + 1) * ROWS, :]


def weigh(place, partial, columns, powers):
    return pl.pallas_call(
        weigh_body,
        in_specs=[SMEM] + [VMEM] * 3,
        out_specs=(VMEM,) * 3,
        out_shape=(
            pltpu.VMEM((16, ROWS, 2 * WIDTH), jnp.bfloat16),
            jax.ShapeDtypeStruct((ROWS, WIDTH), jnp.float32),
            jax.ShapeDtypeStruct((8, WIDTH), jnp.float32),
        ),
        scratch_shapes=[
            pltpu.VMEM((SPAN, WIDTH), jnp.float32),
            pltpu.VMEM((SPAN, 2 * WIDTH), jnp.bfloat16),
        ],
        compiler_params=params(20),
        name="weigh",
    )(place, partial, columns, powers)


def gradient_body(
    core_ref, arrived_ref, inverse_ref, pair_ref, projected_ref, hidden_ref, derivative_ref, own_ref, other_ref
):
    sums = jnp.sum(arrived_ref[...].astype(jnp.float32), axis=0)
    mixed = inverse_ref[...] * sums[:, :WIDTH] + sums[:, WIDTH:]
    derivative = inverse_tau * (mixed - 2.0 * pair_ref[...])
    derivative_ref[...] = derivative
    projected = projected_ref[...]
    inverse_norm = lax.rsqrt(jnp.sum(projected * projected, axis=1, keepdims=True) + norm_epsilon)
    unit = projected * inverse_norm
    alongside = jnp.sum(unit * derivative, axis=1, keepdims=True)
    projected_grad = ((derivative - unit * alongside) * inverse_norm).astype(jnp.bfloat16)

    def product(half):
        columns = pl.ds(pl.multiple_of(half * HALF, HALF), HALF)
        return lax.dot_general(
            hidden_ref[:, columns], projected_grad, (((0,), (0,)), ((), ())), preferred_element_type=jnp.float32
        )

    own_ref[...] = product(core_ref[0])
    other_ref[...] = product(1 - core_ref[0]).astype(jnp.bfloat16)


def gradient(core, arrived, inverse, pair, projected, hidden):
    return pl.pallas_call(
        gradient_body,
        in_specs=[SMEM] + [VMEM] * 5,
        out_specs=(VMEM,) * 3,
        out_shape=(
            jax.ShapeDtypeStruct((ROWS, WIDTH), jnp.float32),
            pltpu.VMEM((HALF, WIDTH), jnp.float32),
            pltpu.VMEM((HALF, WIDTH), jnp.bfloat16),
        ),
        compiler_params=params(16),
        name="gradient",
    )(core, arrived, inverse, pair, projected, hidden)


def join_body(own_ref, other_ref, sum_ref):
    for k in range(16):
        part = slice(k * SHARE, (k + 1) * SHARE)
        sum_ref[k] = (own_ref[part, :] + other_ref[part, :].astype(jnp.float32)).astype(jnp.bfloat16)


def join(own, other):
    return pl.pallas_call(
        join_body,
        in_specs=[VMEM] * 2,
        out_specs=VMEM,
        out_shape=pltpu.VMEM((16, SHARE, WIDTH), jnp.bfloat16),
        compiler_params=params(4),
        name="join",
    )(own, other)


def share_body(arrived_ref, copies_ref):
    total = jnp.sum(arrived_ref[...].astype(jnp.float32), axis=0).astype(jnp.bfloat16)
    for k in range(8):
        copies_ref[k] = total


def share(arrived):
    return pl.pallas_call(
        share_body,
        in_specs=[VMEM],
        out_specs=VMEM,
        out_shape=pltpu.VMEM((8, SHARE, WIDTH), jnp.bfloat16),
        compiler_params=params(4),
        name="share",
    )(arrived)


def packet_body(arrived_ref, loss_ref, copies_ref):
    total = jnp.sum(arrived_ref[...].astype(jnp.float32), axis=0).astype(jnp.bfloat16)
    loss = jnp.broadcast_to(loss_ref[0:1, :], (16, WIDTH))
    high = loss.astype(jnp.bfloat16).astype(jnp.float32)
    middle = (loss - high).astype(jnp.bfloat16).astype(jnp.float32)
    low = loss - high - middle
    row = lax.broadcasted_iota(jnp.int32, (16, WIDTH), 0)
    pieces = jnp.where(row == 0, high, jnp.where(row == 1, middle, jnp.where(row == 2, low, 0.0)))
    pieces = pieces.astype(jnp.bfloat16)
    for k in range(16):
        copies_ref[k, :SHARE, :] = total
        copies_ref[k, SHARE:, :] = pieces


def packet(arrived, loss):
    return pl.pallas_call(
        packet_body,
        in_specs=[VMEM] * 2,
        out_specs=VMEM,
        out_shape=pltpu.VMEM((16, SHARE + 16, WIDTH), jnp.bfloat16),
        compiler_params=params(8),
        name="packet",
    )(arrived, loss)


def finish_body(arrived_ref, loss_ref, grad_ref):
    for k in range(32):
        grad_ref[k] = arrived_ref[k, :SHARE, :].astype(jnp.float32)
    pieces = jnp.sum(arrived_ref[:, SHARE:, :].astype(jnp.float32), axis=0)
    loss_ref[...] = jnp.sum(pieces[:, 0:1], axis=0, keepdims=True) * (0.5 / (256 * ROWS))


def finish(arrived):
    return pl.pallas_call(
        finish_body,
        in_specs=[VMEM],
        out_specs=(VMEM, VMEM),
        out_shape=(
            jax.ShapeDtypeStruct((1, 1), jnp.float32),
            jax.ShapeDtypeStruct((32, SHARE, WIDTH), jnp.float32),
        ),
        compiler_params=params(8),
        name="finish",
    )(arrived)


def local(hidden, weight, partner):
    plane_place = (lax.axis_index("xl") * 2 + lax.axis_index("xh")) * 4 + lax.axis_index("y")
    column_place = lax.axis_index("z") * 2 + lax.axis_index("c")
    core = lax.axis_index("c").astype(jnp.int32).reshape(1)
    place = jnp.stack([plane_place, column_place]).astype(jnp.int32)

    projected, features, copies, pair, pair_sum = project(hidden, weight, partner)
    columns = lax.all_gather(features, COLUMN, axis=0, tiled=True)
    rows = lax.all_to_all(copies, PLANE, 0, 0)
    powers, sums = score(place, rows, columns, pair_sum)
    sums = spread(lax.all_gather(sums, "c", axis=0, tiled=True))
    partial = lax.all_to_all(sums, "z", 0, 0)
    weighed, inverse, loss = weigh(place, partial, columns, powers)
    arrived = lax.all_to_all(weighed, PLANE, 0, 0)
    derivative, own, other = gradient(core, arrived, inverse, pair, projected, hidden)
    other = lax.ppermute(other, "c", [(0, 1), (1, 0)])
    shares = lax.all_to_all(join(own, other), PLANE, 0, 0)
    shares = lax.all_to_all(share(shares), "z", 0, 0)
    packets = lax.all_to_all(packet(shares, loss), PLANE, 0, 0)
    packets = lax.all_gather(packets, "c", axis=0, tiled=True)
    mean_loss, grad_weight = finish(packets)
    return (mean_loss.reshape(()), derivative, grad_weight.reshape(D_IN, WIDTH))


def solution(mesh):
    split = Mesh(mesh.devices.reshape(4, 2, 2, 8, 2), AXES)
    return jax.shard_map(
        local,
        mesh=split,
        in_specs=(P(AXES, None), P(), P(AXES)),
        out_specs=(P(), P(AXES, None), P()),
        check_vma=False,
    )
```

```python
import jax
import jax.numpy as jnp
from jax import lax
from jax.experimental import pallas as pl
from jax.experimental.pallas import tpu as pltpu
from jax.sharding import Mesh
from jax.sharding import PartitionSpec as P

inverse_tau = 10.0
norm_epsilon = 1e-06
log2_e = 1.4426950408889634

AXES = ("y", "xl", "c", "z", "xh")
PLANE = ("y", "xl", "xh")
COLUMN = ("z", "c")
ROWS = 192
WIDTH = 128
D_IN = 2048
SPAN = 16 * ROWS
TILES = SPAN // WIDTH
SHARE = D_IN // 32
HALF = D_IN // 2
PIECES = 2
MEBI = 1024 * 1024

VMEM = pl.BlockSpec(memory_space=pltpu.VMEM)
SMEM = pl.BlockSpec(memory_space=pltpu.SMEM)
ANY = pl.BlockSpec(memory_space=pl.ANY)


def params(size):
    return pltpu.CompilerParams(vmem_limit_bytes=size * MEBI)


def total_of(values):
    return jnp.sum(jnp.sum(values, axis=1, keepdims=True), axis=0, keepdims=True)


def project_body(
    hidden_hbm, weight_hbm, partner_hbm, projected_ref, features_ref, copies_ref, pair_ref, pair_sum_ref,
    hidden, weight, partner, hidden_done, weight_done, partner_done,
):
    depth = D_IN // PIECES
    copies = []
    for k in range(PIECES):
        part = slice(k * depth, (k + 1) * depth)
        copies.append(
            (
                pltpu.make_async_copy(hidden_hbm.at[:, part], hidden.at[:, part], hidden_done.at[k]),
                pltpu.make_async_copy(weight_hbm.at[part, :], weight.at[part, :], weight_done.at[k]),
            )
        )
    partner_copy = pltpu.make_async_copy(partner_hbm, partner, partner_done)
    for first, second in copies:
        first.start()
        second.start()
    partner_copy.start()
    projected = jnp.zeros((ROWS, WIDTH), jnp.float32)
    for k in range(PIECES):
        part = slice(k * depth, (k + 1) * depth)
        for copy in copies[k]:
            copy.wait()
        projected += jnp.dot(hidden[:, part], weight[part, :], preferred_element_type=jnp.float32)
    inverse_norm = lax.rsqrt(jnp.sum(projected * projected, axis=1, keepdims=True) + norm_epsilon)
    features = (projected * inverse_norm).astype(jnp.bfloat16)
    features_ref[...] = features
    for k in range(16):
        copies_ref[k] = features
    partner_copy.wait()
    places = lax.rem(partner[...], ROWS)
    picks = lax.broadcasted_iota(jnp.int32, (ROWS, ROWS), 0) == places
    paired = jnp.dot(
        jnp.where(picks, 1.0, 0.0).astype(jnp.bfloat16), features, preferred_element_type=jnp.float32
    )
    projected_ref[...] = projected
    pair_ref[...] = paired
    total = total_of(features.astype(jnp.float32) * paired)
    pair_sum_ref[...] = jnp.broadcast_to(inverse_tau * total, (8, WIDTH))


def project(hidden, weight, partner):
    return pl.pallas_call(
        project_body,
        in_specs=[ANY] * 3,
        out_specs=(VMEM,) * 5,
        out_shape=(
            jax.ShapeDtypeStruct((ROWS, WIDTH), jnp.float32),
            jax.ShapeDtypeStruct((ROWS, WIDTH), jnp.bfloat16),
            pltpu.VMEM((16, ROWS, WIDTH), jnp.bfloat16),
            jax.ShapeDtypeStruct((ROWS, WIDTH), jnp.float32),
            jax.ShapeDtypeStruct((8, WIDTH), jnp.float32),
        ),
        scratch_shapes=[
            pltpu.VMEM((ROWS, D_IN), jnp.bfloat16),
            pltpu.VMEM((D_IN, WIDTH), jnp.bfloat16),
            pltpu.VMEM((1, ROWS), jnp.int32),
            pltpu.SemaphoreType.DMA((PIECES,)),
            pltpu.SemaphoreType.DMA((PIECES,)),
            pltpu.SemaphoreType.DMA,
        ],
        compiler_params=params(60),
        name="project",
    )(hidden, weight, partner.reshape(1, ROWS))


def score_body(place_ref, rows_ref, columns_ref, pair_sum_ref, powers_ref, sums_ref, left, right):
    for b in range(16):
        shard = rows_ref[lax.rem(place_ref[0] + b, 16)]
        scaled = shard.astype(jnp.float32) * (inverse_tau * log2_e)
        high = scaled.astype(jnp.bfloat16)
        left[b * ROWS : (b + 1) * ROWS, :WIDTH] = high
        left[b * ROWS : (b + 1) * ROWS, WIDTH:] = (scaled - high.astype(jnp.float32)).astype(jnp.bfloat16)
    chunk = 2 * WIDTH
    for n in range(SPAN // chunk):
        columns = slice(n * chunk, (n + 1) * chunk)
        piece = jnp.transpose(columns_ref[columns, :])
        right[:WIDTH, columns] = piece
        right[WIDTH:, columns] = piece
    for n in range(SPAN // chunk):
        columns = slice(n * chunk, (n + 1) * chunk)
        powers = jnp.exp2(jnp.dot(left[...], right[:, columns], preferred_element_type=jnp.float32))
        own_row = lax.broadcasted_iota(jnp.int32, (ROWS, chunk), 0) + place_ref[1] * ROWS
        own_column = lax.broadcasted_iota(jnp.int32, (ROWS, chunk), 1) + n * chunk
        first = jnp.where(own_row == own_column, 0.0, powers[:ROWS, :])
        rest = powers[ROWS:, :]
        powers_ref[:ROWS, columns] = first.astype(jnp.bfloat16)
        powers_ref[ROWS:, columns] = rest.astype(jnp.bfloat16)
        sums = jnp.sum(first.reshape(ROWS // 8, 8, chunk), axis=0)
        sums += jnp.sum(rest.reshape((SPAN - ROWS) // 8, 8, chunk), axis=0)
        sums = jnp.sum(sums, axis=0, keepdims=True)
        for half in range(2):
            sums_ref[2 * n + half : 2 * n + half + 1, :] = sums[:, half * WIDTH : (half + 1) * WIDTH]
    sums_ref[TILES:, :] = pair_sum_ref[...]


def score(place, rows, columns, pair_sum):
    return pl.pallas_call(
        score_body,
        in_specs=[SMEM] + [VMEM] * 3,
        out_specs=(VMEM, VMEM),
        out_shape=(
            pltpu.VMEM((SPAN, SPAN), jnp.bfloat16),
            pltpu.VMEM((TILES + 8, WIDTH), jnp.float32),
        ),
        scratch_shapes=[
            pltpu.VMEM((SPAN, 2 * WIDTH), jnp.bfloat16),
            pltpu.VMEM((2 * WIDTH, SPAN), jnp.bfloat16),
        ],
        compiler_params=params(20),
        name="score",
    )(place, rows, columns, pair_sum)


def spread_body(arrived_ref, copies_ref):
    total = arrived_ref[: TILES + 8, :] + arrived_ref[TILES + 8 :, :]
    for k in range(8):
        copies_ref[k] = total


def spread(arrived):
    return pl.pallas_call(
        spread_body,
        in_specs=[VMEM],
        out_specs=VMEM,
        out_shape=pltpu.VMEM((8, TILES + 8, WIDTH), jnp.float32),
        compiler_params=params(4),
        name="spread",
    )(arrived)


def weigh_body(place_ref, partial_ref, columns_ref, powers_ref, out_ref, own_ref, loss_ref, inverse, both):
    sums = jnp.sum(partial_ref[...], axis=0)
    totals = sums[:TILES, :]
    loss_ref[...] = total_of(jnp.log(totals)) - sums[TILES:, :]
    inverses = 1.0 / totals
    for k in range(TILES):
        rows = slice(k * WIDTH, (k + 1) * WIDTH)
        turned = jnp.transpose(jnp.broadcast_to(inverses[k : k + 1, :], (WIDTH, WIDTH)))
        inverse[rows, :] = turned
        piece = columns_ref[rows, :]
        both[rows, :WIDTH] = piece
        both[rows, WIDTH:] = (piece.astype(jnp.float32) * turned).astype(jnp.bfloat16)
    own_ref[...] = inverse[pl.ds(pl.multiple_of(place_ref[1] * ROWS, ROWS), ROWS), :]
    block = 4 * ROWS
    for i in range(SPAN // block):
        weighed = jnp.dot(
            powers_ref[i * block : (i + 1) * block, :], both[...], preferred_element_type=jnp.float32
        ).astype(jnp.bfloat16)
        for b in range(4):
            out_ref[lax.rem(place_ref[0] + 4 * i + b, 16)] = weighed[b * ROWS : (b + 1) * ROWS, :]


def weigh(place, partial, columns, powers):
    return pl.pallas_call(
        weigh_body,
        in_specs=[SMEM] + [VMEM] * 3,
        out_specs=(VMEM,) * 3,
        out_shape=(
            pltpu.VMEM((16, ROWS, 2 * WIDTH), jnp.bfloat16),
            jax.ShapeDtypeStruct((ROWS, WIDTH), jnp.float32),
            jax.ShapeDtypeStruct((8, WIDTH), jnp.float32),
        ),
        scratch_shapes=[
            pltpu.VMEM((SPAN, WIDTH), jnp.float32),
            pltpu.VMEM((SPAN, 2 * WIDTH), jnp.bfloat16),
        ],
        compiler_params=params(20),
        name="weigh",
    )(place, partial, columns, powers)


def half_product(half, hidden_ref, projected_grad):
    columns = pl.ds(pl.multiple_of(half * HALF, HALF), HALF)
    return lax.dot_general(
        hidden_ref[:, columns], projected_grad, (((0,), (0,)), ((), ())), preferred_element_type=jnp.float32
    )


def gradient_body(
    core_ref, arrived_ref, inverse_ref, pair_ref, projected_ref, hidden_ref, derivative_ref, turned_ref, other_ref
):
    sums = jnp.sum(arrived_ref[...].astype(jnp.float32), axis=0)
    mixed = inverse_ref[...] * sums[:, :WIDTH] + sums[:, WIDTH:]
    derivative = inverse_tau * (mixed - 2.0 * pair_ref[...])
    derivative_ref[...] = derivative
    projected = projected_ref[...]
    inverse_norm = lax.rsqrt(jnp.sum(projected * projected, axis=1, keepdims=True) + norm_epsilon)
    unit = projected * inverse_norm
    alongside = jnp.sum(unit * derivative, axis=1, keepdims=True)
    projected_grad = ((derivative - unit * alongside) * inverse_norm).astype(jnp.bfloat16)

    turned_ref[...] = projected_grad
    other_ref[...] = half_product(1 - core_ref[0], hidden_ref, projected_grad).astype(jnp.bfloat16)


def own_half_body(core_ref, derivative_ref, turned_ref, hidden_ref, out_ref, own_ref):
    out_ref[...] = derivative_ref[...]
    own_ref[...] = half_product(core_ref[0], hidden_ref, turned_ref[...])


def own_half(core, derivative, turned, hidden):
    return pl.pallas_call(
        own_half_body,
        in_specs=[SMEM] + [VMEM] * 3,
        out_specs=(VMEM, VMEM),
        out_shape=(
            pltpu.HBM((ROWS, WIDTH), jnp.float32),
            pltpu.VMEM((HALF, WIDTH), jnp.float32),
        ),
        compiler_params=params(16),
        name="own_half",
        cost_estimate=pl.CostEstimate(
            flops=2 * ROWS * HALF * WIDTH, bytes_accessed=4 * ROWS * D_IN, transcendentals=0
        ),
    )(core, derivative, turned, hidden)


def gradient(core, arrived, inverse, pair, projected, hidden):
    return pl.pallas_call(
        gradient_body,
        in_specs=[SMEM] + [VMEM] * 5,
        out_specs=(VMEM,) * 3,
        out_shape=(
            pltpu.VMEM((ROWS, WIDTH), jnp.float32),
            pltpu.VMEM((ROWS, WIDTH), jnp.bfloat16),
            pltpu.VMEM((HALF, WIDTH), jnp.bfloat16),
        ),
        compiler_params=params(16),
        name="gradient",
    )(core, arrived, inverse, pair, projected, hidden)


def join_body(own_ref, other_ref, sum_ref):
    for k in range(16):
        part = slice(k * SHARE, (k + 1) * SHARE)
        sum_ref[k] = (own_ref[part, :] + other_ref[part, :].astype(jnp.float32)).astype(jnp.bfloat16)


def join(own, other):
    return pl.pallas_call(
        join_body,
        in_specs=[VMEM] * 2,
        out_specs=VMEM,
        out_shape=pltpu.VMEM((16, SHARE, WIDTH), jnp.bfloat16),
        compiler_params=params(4),
        name="join",
    )(own, other)


def share_body(arrived_ref, copies_ref):
    total = jnp.sum(arrived_ref[...].astype(jnp.float32), axis=0).astype(jnp.bfloat16)
    for k in range(8):
        copies_ref[k] = total


def share(arrived):
    return pl.pallas_call(
        share_body,
        in_specs=[VMEM],
        out_specs=VMEM,
        out_shape=pltpu.VMEM((8, SHARE, WIDTH), jnp.bfloat16),
        compiler_params=params(4),
        name="share",
    )(arrived)


def packet_body(arrived_ref, loss_ref, copies_ref):
    total = jnp.sum(arrived_ref[...].astype(jnp.float32), axis=0).astype(jnp.bfloat16)
    loss = jnp.broadcast_to(loss_ref[0:1, :], (16, WIDTH))
    high = loss.astype(jnp.bfloat16).astype(jnp.float32)
    middle = (loss - high).astype(jnp.bfloat16).astype(jnp.float32)
    low = loss - high - middle
    row = lax.broadcasted_iota(jnp.int32, (16, WIDTH), 0)
    pieces = jnp.where(row == 0, high, jnp.where(row == 1, middle, jnp.where(row == 2, low, 0.0)))
    pieces = pieces.astype(jnp.bfloat16)
    for k in range(16):
        copies_ref[k, :SHARE, :] = total
        copies_ref[k, SHARE:, :] = pieces


def packet(arrived, loss):
    return pl.pallas_call(
        packet_body,
        in_specs=[VMEM] * 2,
        out_specs=VMEM,
        out_shape=pltpu.VMEM((16, SHARE + 16, WIDTH), jnp.bfloat16),
        compiler_params=params(8),
        name="packet",
    )(arrived, loss)


def finish_body(arrived_ref, loss_ref, grad_ref):
    for k in range(32):
        grad_ref[k] = arrived_ref[k, :SHARE, :].astype(jnp.float32)
    pieces = jnp.sum(arrived_ref[:, SHARE:, :].astype(jnp.float32), axis=0)
    loss_ref[...] = jnp.sum(pieces[:, 0:1], axis=0, keepdims=True) * (0.5 / (256 * ROWS))


def finish(arrived):
    return pl.pallas_call(
        finish_body,
        in_specs=[VMEM],
        out_specs=(VMEM, VMEM),
        out_shape=(
            jax.ShapeDtypeStruct((1, 1), jnp.float32),
            jax.ShapeDtypeStruct((32, SHARE, WIDTH), jnp.float32),
        ),
        compiler_params=params(8),
        name="finish",
    )(arrived)


def local(hidden, weight, partner):
    plane_place = (lax.axis_index("y") * 2 + lax.axis_index("xl")) * 2 + lax.axis_index("xh")
    column_place = lax.axis_index("z") * 2 + lax.axis_index("c")
    core = lax.axis_index("c").astype(jnp.int32).reshape(1)
    place = jnp.stack([plane_place, column_place]).astype(jnp.int32)

    projected, features, copies, pair, pair_sum = project(hidden, weight, partner)
    columns = lax.all_gather(features, COLUMN, axis=0, tiled=True)
    rows = lax.all_to_all(copies, PLANE, 0, 0)
    powers, sums = score(place, rows, columns, pair_sum)
    sums = spread(lax.all_gather(sums, "c", axis=0, tiled=True))
    partial = lax.all_to_all(sums, "z", 0, 0)
    weighed, inverse, loss = weigh(place, partial, columns, powers)
    arrived = lax.all_to_all(weighed, PLANE, 0, 0)
    derivative, turned, other = gradient(core, arrived, inverse, pair, projected, hidden)
    other = lax.ppermute(other, "c", [(0, 1), (1, 0)])
    derivative, own = own_half(core, derivative, turned, hidden)
    shares = lax.all_to_all(join(own, other), PLANE, 0, 0)
    shares = lax.all_to_all(share(shares), "z", 0, 0)
    packets = lax.all_to_all(packet(shares, loss), PLANE, 0, 0)
    packets = lax.all_gather(packets, "c", axis=0, tiled=True)
    mean_loss, grad_weight = finish(packets)
    return (mean_loss.reshape(()), derivative, grad_weight.reshape(D_IN, WIDTH))


def solution(mesh):
    split = Mesh(mesh.devices.reshape(4, 2, 2, 8, 2), AXES)
    return jax.shard_map(
        local,
        mesh=split,
        in_specs=(P(AXES, None), P(), P(AXES)),
        out_specs=(P(), P(AXES, None), P()),
        check_vma=False,
    )
```

```python
import jax
import jax.numpy as jnp
from jax import lax
from jax.experimental import pallas as pl
from jax.experimental.pallas import tpu as pltpu
from jax.sharding import Mesh
from jax.sharding import PartitionSpec as P

inverse_tau = 10.0
norm_epsilon = 1e-06
log2_e = 1.4426950408889634

AXES = ("y", "xl", "c", "z", "xh")
PLANE = ("y", "xl", "xh")
COLUMN = ("z", "c")
ROWS = 192
WIDTH = 128
D_IN = 2048
SPAN = 16 * ROWS
TILES = SPAN // WIDTH
SHARE = D_IN // 32
HALF = D_IN // 2
PIECES = 2
MEBI = 1024 * 1024

VMEM = pl.BlockSpec(memory_space=pltpu.VMEM)
SMEM = pl.BlockSpec(memory_space=pltpu.SMEM)
ANY = pl.BlockSpec(memory_space=pl.ANY)


def params(size):
    return pltpu.CompilerParams(vmem_limit_bytes=size * MEBI)


def total_of(values):
    return jnp.sum(jnp.sum(values, axis=1, keepdims=True), axis=0, keepdims=True)


def project_body(
    hidden_hbm, weight_hbm, partner_hbm, projected_ref, features_ref, copies_ref, pair_ref, pair_sum_ref,
    hidden, weight, partner, hidden_done, weight_done, partner_done,
):
    depth = D_IN // PIECES
    copies = []
    for k in range(PIECES):
        part = slice(k * depth, (k + 1) * depth)
        copies.append(
            (
                pltpu.make_async_copy(hidden_hbm.at[:, part], hidden.at[:, part], hidden_done.at[k]),
                pltpu.make_async_copy(weight_hbm.at[part, :], weight.at[part, :], weight_done.at[k]),
            )
        )
    partner_copy = pltpu.make_async_copy(partner_hbm, partner, partner_done)
    for first, second in copies:
        first.start()
        second.start()
    partner_copy.start()
    projected = jnp.zeros((ROWS, WIDTH), jnp.float32)
    for k in range(PIECES):
        part = slice(k * depth, (k + 1) * depth)
        for copy in copies[k]:
            copy.wait()
        projected += jnp.dot(hidden[:, part], weight[part, :], preferred_element_type=jnp.float32)
    inverse_norm = lax.rsqrt(jnp.sum(projected * projected, axis=1, keepdims=True) + norm_epsilon)
    features = (projected * inverse_norm).astype(jnp.bfloat16)
    features_ref[...] = features
    for k in range(16):
        copies_ref[k] = features
    partner_copy.wait()
    places = lax.rem(partner[...], ROWS)
    picks = lax.broadcasted_iota(jnp.int32, (ROWS, ROWS), 0) == places
    paired = jnp.dot(
        jnp.where(picks, 1.0, 0.0).astype(jnp.bfloat16), features, preferred_element_type=jnp.float32
    )
    projected_ref[...] = projected
    pair_ref[...] = paired
    total = total_of(features.astype(jnp.float32) * paired)
    pair_sum_ref[...] = jnp.broadcast_to(inverse_tau * total, (8, WIDTH))


def project(hidden, weight, partner):
    return pl.pallas_call(
        project_body,
        in_specs=[ANY] * 3,
        out_specs=(VMEM,) * 5,
        out_shape=(
            jax.ShapeDtypeStruct((ROWS, WIDTH), jnp.float32),
            jax.ShapeDtypeStruct((ROWS, WIDTH), jnp.bfloat16),
            pltpu.VMEM((16, ROWS, WIDTH), jnp.bfloat16),
            jax.ShapeDtypeStruct((ROWS, WIDTH), jnp.float32),
            jax.ShapeDtypeStruct((8, WIDTH), jnp.float32),
        ),
        scratch_shapes=[
            pltpu.VMEM((ROWS, D_IN), jnp.bfloat16),
            pltpu.VMEM((D_IN, WIDTH), jnp.bfloat16),
            pltpu.VMEM((1, ROWS), jnp.int32),
            pltpu.SemaphoreType.DMA((PIECES,)),
            pltpu.SemaphoreType.DMA((PIECES,)),
            pltpu.SemaphoreType.DMA,
        ],
        compiler_params=params(60),
        name="project",
    )(hidden, weight, partner.reshape(1, ROWS))


def score_body(place_ref, rows_ref, columns_ref, pair_sum_ref, powers_ref, sums_ref, left, right):
    for b in range(16):
        shard = rows_ref[lax.rem(place_ref[0] + b, 16)]
        scaled = shard.astype(jnp.float32) * (inverse_tau * log2_e)
        high = scaled.astype(jnp.bfloat16)
        left[b * ROWS : (b + 1) * ROWS, :WIDTH] = high
        left[b * ROWS : (b + 1) * ROWS, WIDTH:] = (scaled - high.astype(jnp.float32)).astype(jnp.bfloat16)
    chunk = 2 * WIDTH
    for n in range(SPAN // chunk):
        columns = slice(n * chunk, (n + 1) * chunk)
        piece = jnp.transpose(columns_ref[columns, :])
        right[:WIDTH, columns] = piece
        right[WIDTH:, columns] = piece
    for n in range(SPAN // chunk):
        columns = slice(n * chunk, (n + 1) * chunk)
        powers = jnp.exp2(jnp.dot(left[...], right[:, columns], preferred_element_type=jnp.float32))
        own_row = lax.broadcasted_iota(jnp.int32, (ROWS, chunk), 0) + place_ref[1] * ROWS
        own_column = lax.broadcasted_iota(jnp.int32, (ROWS, chunk), 1) + n * chunk
        first = jnp.where(own_row == own_column, 0.0, powers[:ROWS, :])
        rest = powers[ROWS:, :]
        powers_ref[:ROWS, columns] = first.astype(jnp.bfloat16)
        powers_ref[ROWS:, columns] = rest.astype(jnp.bfloat16)
        sums = jnp.sum(first.reshape(ROWS // 8, 8, chunk), axis=0)
        sums += jnp.sum(rest.reshape((SPAN - ROWS) // 8, 8, chunk), axis=0)
        sums = jnp.sum(sums, axis=0, keepdims=True)
        for half in range(2):
            sums_ref[2 * n + half : 2 * n + half + 1, :] = sums[:, half * WIDTH : (half + 1) * WIDTH]
    sums_ref[TILES:, :] = pair_sum_ref[...]


def score(place, rows, columns, pair_sum):
    return pl.pallas_call(
        score_body,
        in_specs=[SMEM] + [VMEM] * 3,
        out_specs=(VMEM, VMEM),
        out_shape=(
            pltpu.VMEM((SPAN, SPAN), jnp.bfloat16),
            pltpu.VMEM((TILES + 8, WIDTH), jnp.float32),
        ),
        scratch_shapes=[
            pltpu.VMEM((SPAN, 2 * WIDTH), jnp.bfloat16),
            pltpu.VMEM((2 * WIDTH, SPAN), jnp.bfloat16),
        ],
        compiler_params=params(20),
        name="score",
    )(place, rows, columns, pair_sum)


def spread_body(arrived_ref, copies_ref):
    total = arrived_ref[: TILES + 8, :] + arrived_ref[TILES + 8 :, :]
    for k in range(8):
        copies_ref[k] = total


def spread(arrived):
    return pl.pallas_call(
        spread_body,
        in_specs=[VMEM],
        out_specs=VMEM,
        out_shape=pltpu.VMEM((8, TILES + 8, WIDTH), jnp.float32),
        compiler_params=params(4),
        name="spread",
    )(arrived)


def weigh_body(place_ref, partial_ref, columns_ref, powers_ref, out_ref, own_ref, loss_ref, inverse, both):
    sums = jnp.sum(partial_ref[...], axis=0)
    totals = sums[:TILES, :]
    loss_ref[...] = total_of(jnp.log(totals)) - sums[TILES:, :]
    inverses = 1.0 / totals
    for k in range(TILES):
        rows = slice(k * WIDTH, (k + 1) * WIDTH)
        turned = jnp.transpose(jnp.broadcast_to(inverses[k : k + 1, :], (WIDTH, WIDTH)))
        inverse[rows, :] = turned
        piece = columns_ref[rows, :]
        both[rows, :WIDTH] = piece
        both[rows, WIDTH:] = (piece.astype(jnp.float32) * turned).astype(jnp.bfloat16)
    own_ref[...] = inverse[pl.ds(pl.multiple_of(place_ref[1] * ROWS, ROWS), ROWS), :]
    block = 4 * ROWS
    for i in range(SPAN // block):
        weighed = jnp.dot(
            powers_ref[i * block : (i + 1) * block, :], both[...], preferred_element_type=jnp.float32
        ).astype(jnp.bfloat16)
        for b in range(4):
            out_ref[lax.rem(place_ref[0] + 4 * i + b, 16)] = weighed[b * ROWS : (b + 1) * ROWS, :]


def weigh(place, partial, columns, powers):
    return pl.pallas_call(
        weigh_body,
        in_specs=[SMEM] + [VMEM] * 3,
        out_specs=(VMEM,) * 3,
        out_shape=(
            pltpu.VMEM((16, ROWS, 2 * WIDTH), jnp.bfloat16),
            jax.ShapeDtypeStruct((ROWS, WIDTH), jnp.float32),
            jax.ShapeDtypeStruct((8, WIDTH), jnp.float32),
        ),
        scratch_shapes=[
            pltpu.VMEM((SPAN, WIDTH), jnp.float32),
            pltpu.VMEM((SPAN, 2 * WIDTH), jnp.bfloat16),
        ],
        compiler_params=params(20),
        name="weigh",
    )(place, partial, columns, powers)


def gradient_body(
    core_ref, arrived_ref, inverse_ref, pair_ref, projected_ref, hidden_ref, derivative_ref, own_ref, other_ref
):
    sums = jnp.sum(arrived_ref[...].astype(jnp.float32), axis=0)
    mixed = inverse_ref[...] * sums[:, :WIDTH] + sums[:, WIDTH:]
    derivative = inverse_tau * (mixed - 2.0 * pair_ref[...])
    derivative_ref[...] = derivative
    projected = projected_ref[...]
    inverse_norm = lax.rsqrt(jnp.sum(projected * projected, axis=1, keepdims=True) + norm_epsilon)
    unit = projected * inverse_norm
    alongside = jnp.sum(unit * derivative, axis=1, keepdims=True)
    projected_grad = ((derivative - unit * alongside) * inverse_norm).astype(jnp.bfloat16)

    def product(half):
        columns = pl.ds(pl.multiple_of(half * HALF, HALF), HALF)
        return lax.dot_general(
            hidden_ref[:, columns], projected_grad, (((0,), (0,)), ((), ())), preferred_element_type=jnp.float32
        )

    own_ref[...] = product(core_ref[0])
    other_ref[...] = product(1 - core_ref[0]).astype(jnp.bfloat16)


def gradient(core, arrived, inverse, pair, projected, hidden):
    return pl.pallas_call(
        gradient_body,
        in_specs=[SMEM] + [VMEM] * 5,
        out_specs=(VMEM,) * 3,
        out_shape=(
            jax.ShapeDtypeStruct((ROWS, WIDTH), jnp.float32),
            pltpu.VMEM((HALF, WIDTH), jnp.float32),
            pltpu.VMEM((HALF, WIDTH), jnp.bfloat16),
        ),
        compiler_params=params(16),
        name="gradient",
    )(core, arrived, inverse, pair, projected, hidden)


def join_body(own_ref, other_ref, loss_ref, sum_ref):
    loss = jnp.broadcast_to(loss_ref[0:1, :], (16, WIDTH))
    high = loss.astype(jnp.bfloat16).astype(jnp.float32)
    middle = (loss - high).astype(jnp.bfloat16).astype(jnp.float32)
    low = loss - high - middle
    row = lax.broadcasted_iota(jnp.int32, (16, WIDTH), 0)
    pieces = jnp.where(row == 0, high, jnp.where(row == 1, middle, jnp.where(row == 2, low, 0.0)))
    pieces = pieces.astype(jnp.bfloat16)
    for k in range(16):
        part = slice(k * SHARE, (k + 1) * SHARE)
        sum_ref[k, SHARE:, :] = pieces
        sum_ref[k, :SHARE, :] = (own_ref[part, :] + other_ref[part, :].astype(jnp.float32)).astype(jnp.bfloat16)


def join(own, other, loss):
    return pl.pallas_call(
        join_body,
        in_specs=[VMEM] * 3,
        out_specs=VMEM,
        out_shape=pltpu.VMEM((16, SHARE + 16, WIDTH), jnp.bfloat16),
        compiler_params=params(4),
        name="join",
    )(own, other, loss)


def share_body(arrived_ref, copies_ref, loss_ref):
    sums = jnp.sum(arrived_ref[...].astype(jnp.float32), axis=0)
    total = sums[:SHARE, :].astype(jnp.bfloat16)
    loss_ref[...] = jnp.sum(sums[SHARE:, 0:1], axis=0, keepdims=True) * (1.0 / (256 * ROWS))
    for k in range(8):
        copies_ref[k] = total


def share(arrived):
    return pl.pallas_call(
        share_body,
        in_specs=[VMEM],
        out_specs=(VMEM, VMEM),
        out_shape=(
            pltpu.VMEM((8, SHARE, WIDTH), jnp.bfloat16),
            jax.ShapeDtypeStruct((1, 1), jnp.float32),
        ),
        compiler_params=params(4),
        name="share",
    )(arrived)


def packet_body(arrived_ref, copies_ref):
    total = jnp.sum(arrived_ref[...].astype(jnp.float32), axis=0).astype(jnp.bfloat16)
    for k in range(16):
        copies_ref[k] = total


def packet(arrived):
    return pl.pallas_call(
        packet_body,
        in_specs=[VMEM],
        out_specs=VMEM,
        out_shape=pltpu.VMEM((16, SHARE, WIDTH), jnp.bfloat16),
        compiler_params=params(8),
        name="packet",
    )(arrived)


def finish_body(arrived_ref, grad_ref):
    for k in range(32):
        grad_ref[k] = arrived_ref[k].astype(jnp.float32)


def finish(arrived):
    return pl.pallas_call(
        finish_body,
        in_specs=[VMEM],
        out_specs=VMEM,
        out_shape=jax.ShapeDtypeStruct((32, SHARE, WIDTH), jnp.float32),
        compiler_params=params(8),
        name="finish",
    )(arrived)


def local(hidden, weight, partner):
    plane_place = (lax.axis_index("y") * 2 + lax.axis_index("xl")) * 2 + lax.axis_index("xh")
    column_place = lax.axis_index("z") * 2 + lax.axis_index("c")
    core = lax.axis_index("c").astype(jnp.int32).reshape(1)
    place = jnp.stack([plane_place, column_place]).astype(jnp.int32)

    projected, features, copies, pair, pair_sum = project(hidden, weight, partner)
    columns = lax.all_gather(features, COLUMN, axis=0, tiled=True)
    rows = lax.all_to_all(copies, PLANE, 0, 0)
    powers, sums = score(place, rows, columns, pair_sum)
    sums = spread(lax.all_gather(sums, "c", axis=0, tiled=True))
    partial = lax.all_to_all(sums, "z", 0, 0)
    weighed, inverse, loss = weigh(place, partial, columns, powers)
    arrived = lax.all_to_all(weighed, PLANE, 0, 0)
    derivative, own, other = gradient(core, arrived, inverse, pair, projected, hidden)
    other = lax.ppermute(other, "c", [(0, 1), (1, 0)])
    shares = lax.all_to_all(join(own, other, loss), PLANE, 0, 0)
    shares, mean_loss = share(shares)
    shares = lax.all_to_all(shares, "z", 0, 0)
    packets = lax.all_to_all(packet(shares), PLANE, 0, 0)
    packets = lax.all_gather(packets, "c", axis=0, tiled=True)
    grad_weight = finish(packets)
    return (mean_loss.reshape(()), derivative, grad_weight.reshape(D_IN, WIDTH))


def solution(mesh):
    split = Mesh(mesh.devices.reshape(4, 2, 2, 8, 2), AXES)
    return jax.shard_map(
        local,
        mesh=split,
        in_specs=(P(AXES, None), P(), P(AXES)),
        out_specs=(P(), P(AXES, None), P()),
        check_vma=False,
    )
```
